256 devices in a mesh: expert: 128 (over x, y, z), dp: 2 (over core).
Axes of the slice: x: 4, y: 4, z: 8, core: 2. Of those that a mesh axis runs over, the one named last changes fastest.
Arguments:
- tokens: bfloat16 [2, 4096, 2048], P('dp', 'expert'), may hold values from -6 to 6
- expert_ids: int32 [2, 4096, 8], P('dp', 'expert'), may hold values from 0 to 127, as said below
- route_weight: float32 [2, 4096, 8], P('dp', 'expert'), may hold values from 0.05 to 0.5
- w_gate_up: bfloat16 [128, 2, 2048, 768], P('expert', None, None, 'dp'), may hold values from -0.125 to 0.125
- w_down: bfloat16 [128, 768, 2048], P('expert', 'dp'), may hold values from -0.21875 to 0.21875
- out_grad: bfloat16 [2, 4096, 2048], P('dp', 'expert'), may hold values from -6 to 6
Outputs:
- layer_out: bfloat16 [2, 4096, 2048], P('dp', 'expert')
- token_grad: bfloat16 [2, 4096, 2048], P('dp', 'expert')
- prob_grad: float32 [2, 4096, 8], P('dp', 'expert')
- grad_gate_up: bfloat16 [128, 2, 2048, 768], P('expert', None, None, 'dp')
- grad_down: bfloat16 [128, 768, 2048], P('expert', 'dp')
The draws below stay inside these ranges and needn't reach their ends.
Inputs may be any that keep to these rules, and one draw needn't show every extreme that they name: `expert_ids`: each token names 8 different experts. Among the 32 tokens of one aligned block of a replica no expert is named more than 4 times, and in every draw some expert is named exactly 4 times in every block of both replicas.
All inputs are finite; a program needn't handle non-finite values.
Results may differ from the reference program's by a relative error of at most 0.0064.
Values may be sent and summed in bfloat16 or wider, within the bound.
No kernel may reach another device: no remote copies, remote signals or barrier semaphores. Data moves between devices by JAX's collectives and lax.ppermute only.
A program may use at most 128 MiB of HBM per device.

```python
import math
import jax
import jax.numpy as jnp
from jax import lax

D = 2048
FF = 768
TOP = 8
TOK_DEV = 32
EXPERTS = 128
REPLICAS = 2
TOKENS = 4096
SLOT = 4


def draw_expert_ids(key, part):
    key_popular, key_hot, key_jitter, key_tier, key_shuffle = jax.random.split(key, 5)
    expert_range = jnp.arange(EXPERTS, dtype=jnp.int32)
    popular = jax.random.randint(key_popular, (EXPERTS,), 0, 4)
    hottest = jax.random.randint(key_hot, (), 0, EXPERTS)
    jitter = jax.random.randint(key_jitter, (REPLICAS, EXPERTS, EXPERTS), 0, 1000)
    scores = (popular * 1000 + jitter) * EXPERTS + expert_range
    scores = jnp.where(expert_range == hottest, 268435456, scores)
    ranked = jnp.argsort(-scores, axis=-1, stable=True)
    rank_of = jnp.argsort(ranked, axis=-1, stable=True)
    top_tier = jax.random.randint(key_tier, (REPLICAS, EXPERTS, 1), max(1, EXPERTS // 16), EXPERTS // 3 + 1)
    counts = jnp.where(rank_of < top_tier, SLOT, jnp.where(rank_of >= EXPERTS - top_tier, 0, SLOT // 2))
    bounds = jnp.cumsum(counts, axis=-1)
    pair_range = jnp.arange(TOK_DEV * TOP, dtype=jnp.int32)
    labels = jnp.sum((bounds[..., :, None] <= pair_range).astype(jnp.int32), axis=-2)
    labels = labels.reshape(REPLICAS, EXPERTS, TOP, TOK_DEV).transpose(0, 1, 3, 2)
    shuffle_keys = jax.random.randint(key_shuffle, (REPLICAS, EXPERTS, TOK_DEV), 0, 1048576) * TOK_DEV + jnp.arange(TOK_DEV, dtype=jnp.int32)
    shuffle = jnp.argsort(shuffle_keys, axis=-1, stable=True)
    shuffled = jnp.take_along_axis(labels, shuffle[..., None], axis=2)
    return shuffled.reshape(REPLICAS, EXPERTS * TOK_DEV, TOP).astype(jnp.int32)


def steps_of(stream_key, dims, shards, least, high):
    gain, own = 1.0, jax.random.fold_in(stream_key, 6)
    for axis_at, blocks in shards:
        heights = jnp.exp(jax.random.uniform(jax.random.fold_in(own, axis_at), (blocks,), jnp.float32, least / len(shards), high / len(shards)))
        gain = gain * jnp.repeat(heights, dims[axis_at] // blocks).reshape([-1 if axis == axis_at else 1 for axis in range(len(dims))])
    return gain


def noise(rng, dims, width, reach, cuts=(), kind=jnp.bfloat16):
    result = jax.random.normal(rng, dims, jnp.float32) * width
    if len(cuts) > 0:
        result = steps_of(rng, dims, cuts, -0.22, 0.18) * result
    return jnp.clip(result, min=-reach, max=reach).astype(kind)


def setup_inputs(seed: int = 0) -> dict:
    seeds = jax.random.split(jax.random.key(seed), 7)
    tokens = noise(seeds[0], (REPLICAS, TOKENS, D), 1.0, 6.0, ((0, 2), (1, 128)))
    expert_ids = draw_expert_ids(jax.random.fold_in(seeds[6], 71), 0)
    route_weight = jnp.clip(jnp.exp(math.log(0.5) - 2.3025851 * jax.random.uniform(seeds[2], (REPLICAS, TOKENS, TOP), jnp.float32) ** steps_of(seeds[2], (REPLICAS, TOKENS, TOP), ((0, 2), (1, 128)), -0.2, 0.2)), 0.05, 0.5)
    w_gate_up = noise(seeds[3], (EXPERTS, 2, D, FF), D ** -0.5, 0.125, ((0, 128), (3, 2)))
    w_down = noise(seeds[4], (EXPERTS, FF, D), FF ** -0.5, 0.21875, ((0, 128), (1, 2)))
    out_grad = noise(seeds[5], (REPLICAS, TOKENS, D), 1.0, 6.0, ((0, 2), (1, 128)))
    return {"tokens": tokens, "expert_ids": expert_ids, "route_weight": route_weight, "w_gate_up": w_gate_up, "w_down": w_down, "out_grad": out_grad}


def slot_places(expert_ids):
    pair_count = TOK_DEV * TOP
    chosen = expert_ids.reshape(REPLICAS, EXPERTS, pair_count)
    onehot = (chosen[..., None] == jnp.arange(EXPERTS, dtype=jnp.int32)).astype(jnp.int32)
    earlier = jnp.cumsum(onehot, axis=2) - onehot
    return (chosen * SLOT + jnp.sum(earlier * onehot, axis=3)).astype(jnp.int32)


def reference(tokens, expert_ids, route_weight, w_gate_up, w_down, out_grad):
    pair_count = TOK_DEV * TOP
    capacity = EXPERTS * SLOT
    places = slot_places(expert_ids)
    replica_ix = jnp.arange(REPLICAS, dtype=jnp.int32)[:, None, None]
    source_ix = jnp.arange(EXPERTS, dtype=jnp.int32)[None, :, None]
    pair_ids = jnp.broadcast_to(jnp.arange(pair_count, dtype=jnp.int32), places.shape)
    slot_table = jnp.full((REPLICAS, EXPERTS, capacity), pair_count, jnp.int32)
    slot_table = slot_table.at[replica_ix, source_ix, places].set(pair_ids)
    token_rows = tokens.reshape(REPLICAS, EXPERTS, TOK_DEV, 1, D)
    grad_rows = out_grad.reshape(REPLICAS, EXPERTS, TOK_DEV, 1, D)
    weight_rows = route_weight.reshape(REPLICAS, EXPERTS, TOK_DEV, TOP, 1)
    x_pairs = jnp.broadcast_to(token_rows, (REPLICAS, EXPERTS, TOK_DEV, TOP, D)).reshape(REPLICAS, EXPERTS, pair_count, D)
    do_pairs = (weight_rows * grad_rows.astype(jnp.float32)).astype(jnp.bfloat16).reshape(REPLICAS, EXPERTS, pair_count, D)
    padding = ((0, 0), (0, 0), (0, 1), (0, 0))
    x_pairs = jnp.pad(x_pairs, padding)
    do_pairs = jnp.pad(do_pairs, padding)

    def one_expert(carried, expert):
        out_pairs, dx_pairs = carried
        picked = lax.dynamic_slice_in_dim(slot_table, expert * SLOT, SLOT, 2)
        rows_in = jnp.take_along_axis(x_pairs, picked[..., None], axis=2).reshape(-1, D)
        rows_grad = jnp.take_along_axis(do_pairs, picked[..., None], axis=2).reshape(-1, D)
        gate_up = w_gate_up[expert]
        weight_down = w_down[expert]
        gate_value = jnp.dot(rows_in, gate_up[0], preferred_element_type=jnp.float32)
        up_value = jnp.dot(rows_in, gate_up[1], preferred_element_type=jnp.float32)
        squash = jax.nn.sigmoid(gate_value)
        hidden = (gate_value * squash * up_value).astype(jnp.bfloat16)
        outputs = jnp.dot(hidden, weight_down, preferred_element_type=jnp.float32).astype(jnp.bfloat16)
        hidden_grad = jnp.dot(rows_grad, weight_down.T, preferred_element_type=jnp.float32)
        gate_grad = (hidden_grad * up_value * squash * (1.0 + gate_value * (1.0 - squash))).astype(jnp.bfloat16)
        up_grad = (hidden_grad * gate_value * squash).astype(jnp.bfloat16)
        paired = jnp.stack([gate_grad, up_grad], axis=1).astype(jnp.float32)
        row_grads = jnp.einsum("rgf,gdf->rd", paired, gate_up.astype(jnp.float32)).astype(jnp.bfloat16)
        proj_grads = jnp.einsum("rd,rgf->gdf", rows_in.astype(jnp.float32), paired).astype(jnp.bfloat16)
        down_grads = jnp.dot(hidden.T, rows_grad, preferred_element_type=jnp.float32).astype(jnp.bfloat16)
        out_pairs = out_pairs.at[replica_ix, source_ix, picked].set(outputs.reshape(REPLICAS, EXPERTS, SLOT, D))
        dx_pairs = dx_pairs.at[replica_ix, source_ix, picked].set(row_grads.reshape(REPLICAS, EXPERTS, SLOT, D))
        return (out_pairs, dx_pairs), (proj_grads, down_grads)

    start_state = (jnp.zeros((REPLICAS, EXPERTS, pair_count + 1, D), jnp.bfloat16),
                   jnp.zeros((REPLICAS, EXPERTS, pair_count + 1, D), jnp.bfloat16))
    (out_pairs, dx_pairs), (grad_gate_up, grad_down) = lax.scan(one_expert, start_state, jnp.arange(EXPERTS, dtype=jnp.int32))
    out_pairs = out_pairs[:, :, :pair_count].reshape(REPLICAS, TOKENS, TOP, D).astype(jnp.float32)
    dx_pairs = dx_pairs[:, :, :pair_count].reshape(REPLICAS, TOKENS, TOP, D).astype(jnp.float32)
    layer_out = jnp.sum(route_weight[..., None] * out_pairs, axis=2).astype(jnp.bfloat16)
    prob_grad = jnp.sum(out_grad.astype(jnp.float32)[:, :, None, :] * out_pairs, axis=3)
    token_grad = jnp.sum(dx_pairs, axis=2).astype(jnp.bfloat16)
    return (layer_out, token_grad, prob_grad, grad_gate_up, grad_down)
```

```python
import functools

import jax
import jax.numpy as jnp
import numpy as np
from jax import lax
from jax.experimental import pallas as pl
from jax.experimental.pallas import tpu as pltpu
from jax.sharding import Mesh, PartitionSpec as P

F32 = jnp.float32
BF16 = jnp.bfloat16
NX, NY, NZ = 4, 4, 8
PLANE = NX * NY
SLOTS = 4
TOP = 8
MIB = 1 << 20


def dot(a, b):
    return jnp.dot(a, b, preferred_element_type=F32)


def dot_nt(a, b):
    return lax.dot_general(a, b, (((1,), (1,)), ((), ())), preferred_element_type=F32)


def dot_tn(a, b):
    return lax.dot_general(a, b, (((0,), (0,)), ((), ())), preferred_element_type=F32)


def split3(v):
    hi = v.astype(BF16)
    rest = v - hi.astype(F32)
    mid = rest.astype(BF16)
    lo = (rest - mid.astype(F32)).astype(BF16)
    return hi, mid, lo


def place(meta, z):
    n = meta.shape[0]
    rows = PLANE * NZ * SLOTS
    turned = meta.T
    ids = turned[0:TOP]
    weights = turned[TOP : 2 * TOP] + turned[2 * TOP : 3 * TOP] + turned[3 * TOP : 4 * TOP]
    expert = (lax.broadcasted_iota(jnp.int32, (PLANE, n), 0) * NZ + z).astype(F32)
    named = jnp.zeros((PLANE, n), F32)
    weight = jnp.zeros((PLANE, n), F32)
    for k in range(TOP):
        hit = ids[k : k + 1] == expert
        named = jnp.where(hit, 1.0, named)
        weight = jnp.where(hit, weights[k : k + 1], weight)
    block = n // NZ
    shift = block.bit_length() - 1
    from_t = lax.broadcasted_iota(jnp.int32, (n, n), 0)
    to_t = lax.broadcasted_iota(jnp.int32, (n, n), 1)
    same = lax.shift_right_logical(from_t, shift) == lax.shift_right_logical(to_t, shift)
    before = jnp.where(same & (from_t < to_t), 1.0, 0.0).astype(BF16)
    rank = dot(named.astype(BF16), before)
    rank = jnp.where(named > 0.5, rank, -1.0)

    def spread(v):
        return jnp.broadcast_to(v[:, None, :], (PLANE, NZ * SLOTS, n)).reshape(rows, n)

    row = lax.broadcasted_iota(jnp.int32, (rows, n), 0)
    col = lax.broadcasted_iota(jnp.int32, (rows, n), 1)
    row_block = lax.shift_right_logical(row, 2) & (NZ - 1)
    slot = (row & (SLOTS - 1)).astype(F32)
    here = (spread(rank) == slot) & (lax.shift_right_logical(col, shift) == row_block)
    placing = jnp.where(here, 1.0, 0.0)
    row_weight = jnp.sum(jnp.where(here, spread(weight), 0.0), axis=1, keepdims=True)
    return placing, row_weight, ids


def place_tokens_kernel(z_ref, *refs):
    blobs, (x_ref, placing_ref, weight_ref, ids_ref) = refs[:NZ], refs[NZ:]
    d = x_ref.shape[1]
    meta = jnp.concatenate([b[:, d:].astype(F32) for b in blobs], axis=0)
    placing, row_weight, ids = place(meta, z_ref[0])
    placing = placing.astype(BF16)
    placing_ref[...] = placing
    weight_ref[...] = jnp.broadcast_to(row_weight, weight_ref.shape)
    ids_ref[...] = ids
    tokens = jnp.concatenate([b[:, :d] for b in blobs], axis=0)
    x_ref[...] = dot(placing, tokens).astype(BF16)


def place_grads_kernel(placing_ref, weight_ref, *refs):
    grads, (g_ref, back_ref, back_hi_ref, back_lo_ref) = refs[:NZ], refs[NZ:]
    placing = placing_ref[...]
    row_weight = weight_ref[:, 0:1]
    og = jnp.concatenate([b[...] for b in grads], axis=0)
    g_ref[...] = (dot(placing, og) * row_weight).astype(BF16)
    full = placing.astype(F32)
    back_ref[...] = full.T.astype(BF16)
    weighted = (full * row_weight).T
    hi = weighted.astype(BF16)
    back_hi_ref[...] = hi
    back_lo_ref[...] = (weighted - hi.astype(F32)).astype(BF16)


def combine_out_kernel(z_ref, o_ref, placing_ref, back_hi_ref, back_lo_ref, ids_ref, *refs):
    grads, outs = refs[:NZ], refs[NZ:]
    rows, d = o_ref.shape
    o = o_ref[...]
    placing = placing_ref[...]
    n = placing.shape[1]
    og = jnp.concatenate([b[...] for b in grads], axis=0)
    dots = jnp.sum(dot(placing, og) * o.astype(F32), axis=1, keepdims=True)
    per_expert = jnp.sum(
        (placing.astype(F32) * dots).reshape(PLANE, rows // PLANE, n), axis=1
    )
    expert = (lax.broadcasted_iota(jnp.int32, (PLANE, n), 0) * NZ + z_ref[0]).astype(F32)
    ids = ids_ref[...]
    probs = jnp.concatenate(
        [
            jnp.sum(jnp.where(ids[k : k + 1] == expert, per_expert, 0.0), axis=0, keepdims=True)
            for k in range(TOP)
        ],
        axis=0,
    )
    hi, mid, lo = split3(probs)
    pieces = jnp.concatenate(
        [hi.astype(F32), mid.astype(F32), lo.astype(F32), jnp.zeros((128 - 3 * TOP, n), F32)],
        axis=0,
    ).T
    total = dot(back_hi_ref[...], o) + dot(back_lo_ref[...], o)
    block = n // NZ
    for b in range(NZ):
        at = slice(b * block, (b + 1) * block)
        outs[b][:, :d] = total[at].astype(outs[b].dtype)
        outs[b][:, d:] = pieces[at].astype(outs[b].dtype)


def combine_grads_kernel(o_ref, back_ref, *outs):
    total = dot(back_ref[...], o_ref[...])
    block = total.shape[0] // NZ
    for b in range(NZ):
        outs[b][...] = total[b * block : (b + 1) * block].astype(outs[b].dtype)


def call(kernel, out_shapes, args, scalars=0, flops=0):
    vmem = pl.BlockSpec(memory_space=pltpu.VMEM)
    smem = pl.BlockSpec(memory_space=pltpu.SMEM)
    shapes = [jax.ShapeDtypeStruct(s, t) for s, t in out_shapes]
    nbytes = sum(a.size * a.dtype.itemsize for a in args)
    nbytes += sum(int(np.prod(s)) * jnp.dtype(t).itemsize for s, t in out_shapes)
    return pl.pallas_call(
        kernel,
        out_shape=shapes,
        in_specs=[smem] * scalars + [vmem] * (len(args) - scalars),
        out_specs=[vmem] * len(shapes),
        compiler_params=pltpu.CompilerParams(vmem_limit_bytes=48 * MIB),
        cost_estimate=pl.CostEstimate(flops=flops, bytes_accessed=nbytes, transcendentals=0),
    )(*args)


ORDER = (0, -1, 1, -2, 2, -3, 3, 4)


def shift_z(v, step):
    return lax.ppermute(v, "z", [(i, (i + step) % NZ) for i in range(NZ)])


def gather_z(own):
    held = {0: own}
    for hop in range(1, 5):
        if hop < 4:
            held[-hop] = shift_z(held[1 - hop], 1)
        held[hop] = shift_z(held[hop - 1], -1)
    return [held[r] for r in ORDER]


FIRST = (4, 3)


def part_types():
    return [BF16 if r in FIRST else F32 for r in ORDER]


def scatter_z(parts):
    part = dict(zip(ORDER, parts))
    down = shift_z(part[4], -1)
    up = shift_z(part[3], 1)
    for hop in (3, 2, 1):
        nxt = (part[-hop] + down.astype(F32)).astype(BF16)
        if hop > 1:
            up = shift_z((part[hop - 1] + up.astype(F32)).astype(BF16), 1)
        down = shift_z(nxt, -1)
    return part[0] + (up.astype(F32) + down.astype(F32))


def swap_dp(v):
    return lax.ppermute(v, "dp", [(0, 1), (1, 0)])


def exchange_plane(rows):
    r, d = rows.shape
    out = lax.all_to_all(
        rows.reshape(PLANE, r // PLANE, d), ("x", "y"), split_axis=0, concat_axis=0, tiled=True
    )
    return out.reshape(r, d)


def on_device(tokens, expert_ids, route_weight, w_gate_up, w_down, out_grad):
    t, d = tokens.shape[1:]
    n = t * NZ
    rows = PLANE * NZ * SLOTS
    z = lax.axis_index("z").astype(jnp.int32).reshape(1)

    weight = route_weight[0]
    hi = lax.reduce_precision(weight, 8, 7)
    mid = lax.reduce_precision(weight - hi, 8, 7)
    lo = lax.reduce_precision(weight - hi - mid, 8, 7)
    meta = jnp.concatenate([expert_ids[0].astype(F32), hi, mid, lo], axis=1).astype(BF16)
    meta = jnp.pad(meta, ((0, 0), (0, 128 - meta.shape[1])))
    blobs = gather_z(jnp.concatenate([tokens[0], meta], axis=1))
    grads = gather_z(out_grad[0])

    gu = (w_gate_up[0], swap_dp(w_gate_up[0]))
    wd = (w_down[0], swap_dp(w_down[0]))

    send_x, placing, row_weight, ids = call(
        place_tokens_kernel,
        [((rows, d), BF16), ((rows, n), BF16), ((rows, 128), F32), ((TOP, n), F32)],
        [z, *blobs],
        scalars=1,
        flops=2 * rows * n * d,
    )
    x = exchange_plane(send_x)
    send_g, back, back_hi, back_lo = call(
        place_grads_kernel,
        [((rows, d), BF16)] + [((n, rows), BF16)] * 3,
        [placing, row_weight, *grads],
        flops=2 * rows * n * d,
    )
    g = exchange_plane(send_g)

    gate = [dot(x, w[0]) for w in gu]
    up = [dot(x, w[1]) for w in gu]
    squash = [jax.nn.sigmoid(v) for v in gate]
    hidden = [(a * s * u).astype(BF16) for a, s, u in zip(gate, squash, up)]
    out_rows = (dot(hidden[0], wd[0]) + dot(hidden[1], wd[1])).astype(BF16)
    o = exchange_plane(out_rows)

    hidden_grad = [dot_nt(g, w) for w in wd]
    gate_grad = [
        (h * u * s * (1.0 + a * (1.0 - s))).astype(BF16)
        for h, u, s, a in zip(hidden_grad, up, squash, gate)
    ]
    up_grad = [(h * a * s).astype(BF16) for h, a, s in zip(hidden_grad, gate, squash)]
    grad_rows = (
        dot_nt(gate_grad[0], gu[0][0])
        + dot_nt(up_grad[0], gu[0][1])
        + dot_nt(gate_grad[1], gu[1][0])
        + dot_nt(up_grad[1], gu[1][1])
    ).astype(BF16)
    dx = exchange_plane(grad_rows)

    away = [
        swap_dp(dot_tn(x, gate_grad[1]).astype(BF16)),
        swap_dp(dot_tn(x, up_grad[1]).astype(BF16)),
        swap_dp(dot_tn(hidden[1], g).astype(BF16)),
    ]
    grad_gate_up = jnp.stack(
        [
            (dot_tn(x, gate_grad[0]) + away[0].astype(F32)).astype(BF16),
            (dot_tn(x, up_grad[0]) + away[1].astype(F32)).astype(BF16),
        ]
    )
    grad_down = (dot_tn(hidden[0], g) + away[2].astype(F32)).astype(BF16)

    types = part_types()
    parts = call(
        combine_out_kernel,
        [((t, d + 128), k) for k in types],
        [z, o, placing, back_hi, back_lo, ids, *grads],
        scalars=1,
        flops=6 * rows * n * d,
    )
    total = scatter_z(parts)
    layer_out = total[:, :d].astype(BF16)
    prob_grad = total[:, d : d + TOP] + (
        total[:, d + TOP : d + 2 * TOP] + total[:, d + 2 * TOP : d + 3 * TOP]
    )
    parts = call(
        combine_grads_kernel,
        [((t, d), k) for k in types],
        [dx, back],
        flops=2 * rows * n * d,
    )
    token_grad = scatter_z(parts).astype(BF16)
    return (
        layer_out[None],
        token_grad[None],
        prob_grad[None],
        grad_gate_up[None],
        grad_down[None],
    )


def solution(mesh):
    fine = Mesh(mesh.devices.reshape(NX, NY, NZ, 2), ("x", "y", "z", "dp"))
    expert = ("x", "y", "z")
    by_token = P("dp", expert, None)
    specs = (by_token, by_token, by_token, P(expert, None, None, "dp"), P(expert, "dp", None))
    return jax.shard_map(
        on_device,
        mesh=fine,
        in_specs=specs + (by_token,),
        out_specs=(by_token, by_token, by_token, specs[3], specs[4]),
        check_vma=False,
    )
```

```python
import functools

import jax
import jax.numpy as jnp
import numpy as np
from jax import lax
from jax.experimental import pallas as pl
from jax.experimental.pallas import tpu as pltpu
from jax.sharding import Mesh, PartitionSpec as P

F32 = jnp.float32
BF16 = jnp.bfloat16
NX, NY, NZ = 4, 4, 8
PLANE = NX * NY
SLOTS = 4
TOP = 8
VMEM = 63 << 20
ROWS = 256
COLUMNS = 256


def dot(a, b):
    return jnp.dot(a, b, preferred_element_type=F32)


def dot_nt(a, b):
    return lax.dot_general(a, b, (((1,), (1,)), ((), ())), preferred_element_type=F32)


def dot_tn(a, b):
    return lax.dot_general(a, b, (((0,), (0,)), ((), ())), preferred_element_type=F32)


def split3(v):
    hi = v.astype(BF16)
    rest = v - hi.astype(F32)
    mid = rest.astype(BF16)
    lo = (rest - mid.astype(F32)).astype(BF16)
    return hi, mid, lo


def place(meta, z):
    n = meta.shape[0]
    rows = PLANE * NZ * SLOTS
    turned = meta.T
    ids = turned[0:TOP]
    weights = turned[TOP : 2 * TOP] + turned[2 * TOP : 3 * TOP] + turned[3 * TOP : 4 * TOP]
    expert = (lax.broadcasted_iota(jnp.int32, (PLANE, n), 0) * NZ + z).astype(F32)
    named = jnp.zeros((PLANE, n), F32)
    weight = jnp.zeros((PLANE, n), F32)
    for k in range(TOP):
        hit = ids[k : k + 1] == expert
        named = jnp.where(hit, 1.0, named)
        weight = jnp.where(hit, weights[k : k + 1], weight)
    block = n // NZ
    shift = block.bit_length() - 1
    from_t = lax.broadcasted_iota(jnp.int32, (n, n), 0)
    to_t = lax.broadcasted_iota(jnp.int32, (n, n), 1)
    same = lax.shift_right_logical(from_t, shift) == lax.shift_right_logical(to_t, shift)
    before = jnp.where(same & (from_t < to_t), 1.0, 0.0).astype(BF16)
    rank = dot(named.astype(BF16), before)
    rank = jnp.where(named > 0.5, rank, -1.0)

    def spread(v):
        return jnp.broadcast_to(v[:, None, :], (PLANE, NZ * SLOTS, n)).reshape(rows, n)

    row = lax.broadcasted_iota(jnp.int32, (rows, n), 0)
    col = lax.broadcasted_iota(jnp.int32, (rows, n), 1)
    row_block = lax.shift_right_logical(row, 2) & (NZ - 1)
    slot = (row & (SLOTS - 1)).astype(F32)
    here = (spread(rank) == slot) & (lax.shift_right_logical(col, shift) == row_block)
    placing = jnp.where(here, 1.0, 0.0)
    row_weight = jnp.sum(jnp.where(here, spread(weight), 0.0), axis=1, keepdims=True)
    return placing, row_weight, ids


def blob_kernel(ids_ref, weight_ref, tokens_ref, blob_ref):
    t, d = tokens_ref.shape
    pieces = [v.astype(F32) for v in split3(weight_ref[...])]
    rest = jnp.zeros((128 - 4 * TOP, t), F32)
    meta = jnp.concatenate([ids_ref[...].astype(F32), *pieces, rest], axis=0)
    blob_ref[:, :d] = tokens_ref[...]
    blob_ref[:, d:] = meta.T.astype(BF16)


def place_tokens_kernel(z_ref, *refs):
    blobs, (x_ref, placing_ref, weight_ref, ids_ref) = refs[:NZ], refs[NZ:]
    d = x_ref.shape[1]
    meta = jnp.concatenate([b[:, d:].astype(F32) for b in blobs], axis=0)
    placing, row_weight, ids = place(meta, z_ref[0])
    placing = placing.astype(BF16)
    placing_ref[...] = placing
    weight_ref[...] = jnp.broadcast_to(row_weight, weight_ref.shape)
    ids_ref[...] = ids
    tokens = jnp.concatenate([b[:, :d] for b in blobs], axis=0)
    x_ref[...] = dot(placing, tokens).astype(BF16)


def place_grads_kernel(placing_ref, weight_ref, *refs):
    grads, (g_ref, back_ref, flat_ref) = refs[:NZ], refs[NZ:]
    placing = placing_ref[...]
    og = jnp.concatenate([b[...] for b in grads], axis=0)
    g_ref[...] = (dot(placing, og) * weight_ref[:, 0:1]).astype(BF16)
    back_ref[...] = placing.astype(F32).T.astype(BF16)
    flat_ref[...] = weight_ref[...].T[0:TOP]


def combine_out_kernel(
    z_ref, o_ref, g_ref, placing_ref, back_ref, weight_ref, flat_ref, ids_ref, *outs
):
    rows, d = o_ref.shape
    o = o_ref[...]
    placing = placing_ref[...]
    n = placing.shape[1]
    row_weight = weight_ref[:, 0:1]
    inverse = jnp.where(row_weight > 0.0, 1.0 / jnp.where(row_weight > 0.0, row_weight, 1.0), 0.0)
    dots = jnp.sum(g_ref[...].astype(F32) * o.astype(F32), axis=1, keepdims=True) * inverse
    per_expert = jnp.sum(
        (placing.astype(F32) * dots).reshape(PLANE, rows // PLANE, n), axis=1
    )
    expert = (lax.broadcasted_iota(jnp.int32, (PLANE, n), 0) * NZ + z_ref[0]).astype(F32)
    ids = ids_ref[...]
    probs = jnp.concatenate(
        [
            jnp.sum(jnp.where(ids[k : k + 1] == expert, per_expert, 0.0), axis=0, keepdims=True)
            for k in range(TOP)
        ],
        axis=0,
    )
    pieces = [v.astype(F32) for v in split3(probs)]
    pieces = jnp.concatenate([*pieces, jnp.zeros((128 - 3 * TOP, n), F32)], axis=0).T
    weighted = back_ref[...].astype(F32) * flat_ref[0:1]
    hi = weighted.astype(BF16)
    lo = (weighted - hi.astype(F32)).astype(BF16)
    total = dot(hi, o) + dot(lo, o)
    block = n // NZ
    for b in range(NZ):
        at = slice(b * block, (b + 1) * block)
        outs[b][:, :d] = total[at].astype(outs[b].dtype)
        outs[b][:, d:] = pieces[at].astype(outs[b].dtype)


def combine_grads_kernel(o_ref, back_ref, *outs):
    total = dot(back_ref[...], o_ref[...])
    block = total.shape[0] // NZ
    for b in range(NZ):
        outs[b][...] = total[b * block : (b + 1) * block].astype(outs[b].dtype)


def forward_kernel(x_ref, gu_a, gu_b, wd_a, wd_b, gate_ref, up_ref, hidden_ref, out_ref):
    f = wd_a.shape[0]
    for row in range(0, x_ref.shape[0], ROWS):
        here = slice(row, row + ROWS)
        x = x_ref[here]
        total = None
        for half, (gu, wd) in enumerate(((gu_a, wd_a), (gu_b, wd_b))):
            at = slice(half * f, (half + 1) * f)
            gate = dot(x, gu[0])
            up = dot(x, gu[1])
            gate_ref[here, at] = gate
            up_ref[here, at] = up
            hidden = (gate * jax.nn.sigmoid(gate) * up).astype(BF16)
            hidden_ref[here, at] = hidden
            part = dot(hidden, wd[...])
            total = part if total is None else total + part
        out_ref[here] = total.astype(BF16)


def backward_kernel(g_ref, gate_ref, up_ref, gu_a, gu_b, wd_a, wd_b, gg_ref, ug_ref, dx_ref):
    f = wd_a.shape[0]
    for row in range(0, g_ref.shape[0], ROWS):
        here = slice(row, row + ROWS)
        g = g_ref[here]
        total = None
        for half, (gu, wd) in enumerate(((gu_a, wd_a), (gu_b, wd_b))):
            at = slice(half * f, (half + 1) * f)
            gate = gate_ref[here, at]
            squash = jax.nn.sigmoid(gate)
            hidden_grad = dot_nt(g, wd[...])
            gate_grad = hidden_grad * up_ref[here, at] * squash * (1.0 + gate * (1.0 - squash))
            gate_grad = gate_grad.astype(BF16)
            up_grad = (hidden_grad * gate * squash).astype(BF16)
            gg_ref[here, at] = gate_grad
            ug_ref[here, at] = up_grad
            part = dot_nt(gate_grad, gu[0]) + dot_nt(up_grad, gu[1])
            total = part if total is None else total + part
        dx_ref[here] = total.astype(BF16)


def weight_grad_kernel(half, x_ref, g_ref, gg_ref, ug_ref, hidden_ref, *refs):
    received, (gu_ref, wd_ref) = refs[:-2], refs[-2:]
    f = wd_ref.shape[0]
    at = slice(half * f, (half + 1) * f)
    for column in range(0, x_ref.shape[1], COLUMNS):
        here = slice(column, column + COLUMNS)
        x = x_ref[:, here]
        for i, grad in enumerate((gg_ref, ug_ref)):
            v = dot_tn(x, grad[:, at])
            if received:
                v = v + received[0][i, here].astype(F32)
            gu_ref[i, here] = v.astype(BF16)
        v = dot_tn(hidden_ref[:, at], g_ref[:, here])
        if received:
            v = v + received[1][:, here].astype(F32)
        wd_ref[:, here] = v.astype(BF16)


def nothing_kernel(first, second, out):
    pass


def cost(flops, args, out_shapes):
    nbytes = sum(a.size * a.dtype.itemsize for a in [*args, *out_shapes])
    return pl.CostEstimate(flops=flops, bytes_accessed=nbytes, transcendentals=0)


class Arriving:
    def __init__(self, ref, copy):
        self.ref, self.copy = ref, copy
        self.shape, self.dtype = ref.shape, ref.dtype

    def __getitem__(self, at):
        if self.copy is not None:
            self.copy.wait()
            self.copy = None
        return self.ref[at]


def staged(kernel, scalars, read, unread, made, *refs):
    smem, rest = refs[:scalars], refs[scalars:]
    ins, rest = rest[:read], rest[read + unread :]
    outs, rest = rest[:made], rest[made:]
    held, made_here, (in_sems, out_sems) = rest[:read], rest[read : read + made], rest[read + made :]
    arriving = []
    for i, (source, here) in enumerate(zip(ins, held)):
        copy = pltpu.make_async_copy(source, here, in_sems.at[i])
        copy.start()
        arriving.append(Arriving(here, copy))
    kernel(*smem, *arriving, *made_here)
    leaving = []
    for i, (here, target) in enumerate(zip(made_here, outs)):
        copy = pltpu.make_async_copy(here, target, out_sems.at[i])
        copy.start()
        leaving.append(copy)
    for buffer in arriving:
        if buffer.copy is not None:
            buffer.copy.wait()
    for copy in leaving:
        copy.wait()


def call(kernel, out_shapes, args, scalars=0, unread=0, flops=0):
    smem = pl.BlockSpec(memory_space=pltpu.SMEM)
    hbm = pl.BlockSpec(memory_space=pltpu.HBM)
    anywhere = pl.BlockSpec(memory_space=pl.ANY)
    shapes = [jax.ShapeDtypeStruct(s, t) for s, t in out_shapes]
    read = len(args) - scalars - unread
    ins = args[scalars : scalars + read]
    return pl.pallas_call(
        functools.partial(staged, kernel, scalars, read, unread, len(shapes)),
        out_shape=shapes,
        in_specs=[smem] * scalars + [hbm] * read + [anywhere] * unread,
        out_specs=[hbm] * len(shapes),
        scratch_shapes=[pltpu.VMEM(a.shape, a.dtype) for a in [*ins, *shapes]]
        + [pltpu.SemaphoreType.DMA((read,)), pltpu.SemaphoreType.DMA((len(shapes),))],
        compiler_params=pltpu.CompilerParams(vmem_limit_bytes=VMEM),
        cost_estimate=cost(flops, args[: scalars + read] if flops else [], shapes if flops else []),
    )(*args)


def forward(x, gu, wd):
    rows, d = x.shape
    f = wd[0].shape[0]
    wide = (rows, 2 * f)
    return call(
        forward_kernel,
        [(wide, F32), (wide, F32), (wide, BF16), ((rows, d), BF16)],
        [x, *gu, *wd],
        flops=12 * rows * d * f,
    )


def backward(g, gate, up, gu, wd):
    rows, d = g.shape
    f = wd[0].shape[0]
    return call(
        backward_kernel,
        [((rows, 2 * f), BF16), ((rows, 2 * f), BF16), ((rows, d), BF16)],
        [g, gate, up, *gu, *wd],
        flops=12 * rows * d * f,
    )


def weight_grads(x, g, gg, ug, hidden, half, received=()):
    rows, d = x.shape
    f = gg.shape[1] // 2
    return call(
        functools.partial(weight_grad_kernel, half),
        [((2, d, f), BF16), ((f, d), BF16)],
        [x, g, gg, ug, hidden, *received],
        flops=0 if received else 6 * rows * d * f,
    )


def after(value, earlier):
    hbm = pl.BlockSpec(memory_space=pl.ANY)
    return pl.pallas_call(
        nothing_kernel,
        out_shape=jax.ShapeDtypeStruct(value.shape, value.dtype),
        in_specs=[hbm, hbm],
        out_specs=hbm,
        input_output_aliases={0: 0},
        cost_estimate=pl.CostEstimate(flops=0, bytes_accessed=0, transcendentals=0),
    )(value, earlier)


ORDER = (0, -1, 1, -2, 2, -3, 3, 4)


def shift_z(v, step):
    return lax.ppermute(v, "z", [(i, (i + step) % NZ) for i in range(NZ)])


def gather_z(own):
    held = {0: own}
    for hop in range(1, 5):
        if hop < 4:
            held[-hop] = shift_z(held[1 - hop], 1)
        held[hop] = shift_z(held[hop - 1], -1)
    return [held[r] for r in ORDER]


FIRST = (4, 3)


def part_types():
    return [BF16 if r in FIRST else F32 for r in ORDER]


def scatter_z(parts):
    part = dict(zip(ORDER, parts))
    down = shift_z(part[4], -1)
    up = shift_z(part[3], 1)
    for hop in (3, 2, 1):
        nxt = (part[-hop] + down.astype(F32)).astype(BF16)
        if hop > 1:
            up = shift_z((part[hop - 1] + up.astype(F32)).astype(BF16), 1)
        down = shift_z(nxt, -1)
    return part[0] + (up.astype(F32) + down.astype(F32))


def swap_dp(v):
    return lax.ppermute(v, "dp", [(0, 1), (1, 0)])


def exchange_plane(rows):
    r, d = rows.shape
    out = lax.all_to_all(
        rows.reshape(PLANE, r // PLANE, d), ("x", "y"), split_axis=0, concat_axis=0, tiled=True
    )
    return out.reshape(r, d)


def on_device(tokens, expert_ids, route_weight, w_gate_up, w_down, out_grad):
    t, d = tokens.shape[1:]
    n = t * NZ
    rows = PLANE * NZ * SLOTS
    z = lax.axis_index("z").astype(jnp.int32).reshape(1)

    gu = (w_gate_up[0], swap_dp(w_gate_up[0]))
    wd = (w_down[0], swap_dp(w_down[0]))
    (blob,) = call(
        blob_kernel, [((t, d + 128), BF16)], [expert_ids[0].T, route_weight[0].T, tokens[0]]
    )
    blobs = gather_z(blob)
    send_x, placing, row_weight, ids = call(
        place_tokens_kernel,
        [((rows, d), BF16), ((rows, n), BF16), ((rows, 128), F32), ((TOP, n), F32)],
        [z, *blobs, gu[1], wd[1]],
        scalars=1,
        unread=2,
        flops=2 * rows * n * d,
    )
    x = exchange_plane(send_x)
    grads = gather_z(out_grad[0])
    send_g, back, flat = call(
        place_grads_kernel,
        [((rows, d), BF16), ((n, rows), BF16), ((TOP, rows), F32)],
        [placing, row_weight, *grads],
        flops=2 * rows * n * d,
    )
    g = exchange_plane(send_g)
    gate, up, hidden, out_rows = forward(x, gu, wd)
    o = exchange_plane(after(out_rows, g))
    gate_grad, up_grad, grad_rows = backward(g, gate, up, gu, wd)
    grad_rows = after(grad_rows, o)
    dx = exchange_plane(grad_rows)

    away = weight_grads(x, g, gate_grad, up_grad, hidden, 1)
    received = [swap_dp(v) for v in away]
    grad_gate_up, grad_down = weight_grads(x, g, gate_grad, up_grad, hidden, 0, received)

    types = part_types()
    parts = call(
        combine_out_kernel,
        [((t, d + 128), k) for k in types],
        [z, o, send_g, placing, back, row_weight, flat, ids, away[0], grad_rows],
        scalars=1,
        unread=2,
        flops=0,
    )
    total = scatter_z(parts)
    layer_out = total[:, :d].astype(BF16)
    prob_grad = total[:, d : d + TOP] + (
        total[:, d + TOP : d + 2 * TOP] + total[:, d + 2 * TOP : d + 3 * TOP]
    )
    parts = call(
        combine_grads_kernel,
        [((t, d), k) for k in types],
        [dx, back, grad_gate_up],
        unread=1,
        flops=2 * rows * n * d,
    )
    token_grad = scatter_z(parts).astype(BF16)
    return (
        layer_out[None],
        token_grad[None],
        prob_grad[None],
        grad_gate_up[None],
        grad_down[None],
    )


def solution(mesh):
    fine = Mesh(mesh.devices.reshape(NX, NY, NZ, 2), ("x", "y", "z", "dp"))
    expert = ("x", "y", "z")
    by_token = P("dp", expert, None)
    specs = (by_token, by_token, by_token, P(expert, None, None, "dp"), P(expert, "dp", None))
    return jax.shard_map(
        on_device,
        mesh=fine,
        in_specs=specs + (by_token,),
        out_specs=(by_token, by_token, by_token, specs[3], specs[4]),
        check_vma=False,
    )
```

```python
import functools

import jax
import jax.numpy as jnp
import numpy as np
from jax import lax
from jax.experimental import pallas as pl
from jax.experimental.pallas import tpu as pltpu
from jax.sharding import Mesh, PartitionSpec as P

F32 = jnp.float32
BF16 = jnp.bfloat16
NX, NY, NZ = 4, 4, 8
PLANE = NX * NY
SLOTS = 4
TOP = 8
MIB = 1 << 20
ROWS = 256
COLUMNS = 1024


def dot(a, b):
    return jnp.dot(a, b, preferred_element_type=F32)


def dot_nt(a, b):
    return lax.dot_general(a, b, (((1,), (1,)), ((), ())), preferred_element_type=F32)


def dot_tn(a, b):
    return lax.dot_general(a, b, (((0,), (0,)), ((), ())), preferred_element_type=F32)


def split3(v):
    hi = v.astype(BF16)
    rest = v - hi.astype(F32)
    mid = rest.astype(BF16)
    lo = (rest - mid.astype(F32)).astype(BF16)
    return hi, mid, lo


def place(meta, z):
    n = meta.shape[0]
    rows = PLANE * NZ * SLOTS
    turned = meta.T
    ids = turned[0:TOP]
    weights = turned[TOP : 2 * TOP] + turned[2 * TOP : 3 * TOP] + turned[3 * TOP : 4 * TOP]
    expert = (lax.broadcasted_iota(jnp.int32, (PLANE, n), 0) * NZ + z).astype(F32)
    named = jnp.zeros((PLANE, n), F32)
    weight = jnp.zeros((PLANE, n), F32)
    for k in range(TOP):
        hit = ids[k : k + 1] == expert
        named = jnp.where(hit, 1.0, named)
        weight = jnp.where(hit, weights[k : k + 1], weight)
    block = n // NZ
    shift = block.bit_length() - 1
    from_t = lax.broadcasted_iota(jnp.int32, (n, n), 0)
    to_t = lax.broadcasted_iota(jnp.int32, (n, n), 1)
    same = lax.shift_right_logical(from_t, shift) == lax.shift_right_logical(to_t, shift)
    before = jnp.where(same & (from_t < to_t), 1.0, 0.0).astype(BF16)
    rank = dot(named.astype(BF16), before)
    rank = jnp.where(named > 0.5, rank, -1.0)

    def spread(v):
        return jnp.broadcast_to(v[:, None, :], (PLANE, NZ * SLOTS, n)).reshape(rows, n)

    row = lax.broadcasted_iota(jnp.int32, (rows, n), 0)
    col = lax.broadcasted_iota(jnp.int32, (rows, n), 1)
    row_block = lax.shift_right_logical(row, 2) & (NZ - 1)
    slot = (row & (SLOTS - 1)).astype(F32)
    here = (spread(rank) == slot) & (lax.shift_right_logical(col, shift) == row_block)
    placing = jnp.where(here, 1.0, 0.0)
    row_weight = jnp.sum(jnp.where(here, spread(weight), 0.0), axis=1, keepdims=True)
    return placing, row_weight, ids


def blob_kernel(ids_ref, weight_ref, tokens_ref, blob_ref):
    t, d = tokens_ref.shape
    pieces = [v.astype(F32) for v in split3(weight_ref[...])]
    rest = jnp.zeros((128 - 4 * TOP, t), F32)
    meta = jnp.concatenate([ids_ref[...].astype(F32), *pieces, rest], axis=0)
    blob_ref[:, :d] = tokens_ref[...]
    blob_ref[:, d:] = meta.T.astype(BF16)


def place_tokens_kernel(z_ref, *refs):
    blobs, (x_ref, placing_ref, weight_ref, ids_ref) = refs[:NZ], refs[NZ:]
    d = x_ref.shape[1]
    meta = jnp.concatenate([b[:, d:].astype(F32) for b in blobs], axis=0)
    placing, row_weight, ids = place(meta, z_ref[0])
    placing = placing.astype(BF16)
    placing_ref[...] = placing
    weight_ref[...] = jnp.broadcast_to(row_weight, weight_ref.shape)
    ids_ref[...] = ids
    tokens = jnp.concatenate([b[:, :d] for b in blobs], axis=0)
    for row in range(0, x_ref.shape[0], ROWS):
        here = slice(row, row + ROWS)
        x_ref[here] = dot(placing[here], tokens).astype(BF16)
        x_ref.send(here)


def place_grads_kernel(*refs):
    grads, (placing_ref, weight_ref, g_ref, back_ref, flat_ref) = refs[:NZ], refs[NZ:]
    placing = placing_ref[...]
    og = jnp.concatenate([b[...] for b in grads], axis=0)
    g_ref[...] = (dot(placing, og) * weight_ref[:, 0:1]).astype(BF16)
    back_ref[...] = placing.astype(F32).T.astype(BF16)
    flat_ref[...] = weight_ref[...].T[0:TOP]


def put_parts(total, outs):
    block = total.shape[0] // NZ
    for b in range(NZ - 1):
        outs[b][...] = total[b * block : (b + 1) * block].astype(outs[b].dtype)
    far = total[(NZ - 1) * block :].astype(BF16)
    half = outs[NZ - 1].shape[1]
    outs[NZ - 1][...] = far[:, :half]
    outs[NZ][...] = far[:, half:]


def combine_out_kernel(
    z_ref, o_ref, g_ref, placing_ref, back_ref, weight_ref, flat_ref, ids_ref, *outs
):
    rows, d = o_ref.shape
    o = o_ref[...]
    placing = placing_ref[...]
    n = placing.shape[1]
    row_weight = weight_ref[:, 0:1]
    inverse = jnp.where(row_weight > 0.0, 1.0 / jnp.where(row_weight > 0.0, row_weight, 1.0), 0.0)
    dots = jnp.sum(g_ref[...].astype(F32) * o.astype(F32), axis=1, keepdims=True) * inverse
    per_expert = jnp.sum(
        (placing.astype(F32) * dots).reshape(PLANE, rows // PLANE, n), axis=1
    )
    expert = (lax.broadcasted_iota(jnp.int32, (PLANE, n), 0) * NZ + z_ref[0]).astype(F32)
    ids = ids_ref[...]
    probs = jnp.concatenate(
        [
            jnp.sum(jnp.where(ids[k : k + 1] == expert, per_expert, 0.0), axis=0, keepdims=True)
            for k in range(TOP)
        ],
        axis=0,
    )
    pieces = [v.astype(F32) for v in split3(probs)]
    pieces = jnp.concatenate([*pieces, jnp.zeros((128 - 3 * TOP, n), F32)], axis=0).T
    weighted = back_ref[...].astype(F32) * flat_ref[0:1]
    hi = weighted.astype(BF16)
    lo = (weighted - hi.astype(F32)).astype(BF16)
    total = dot(hi, o) + dot(lo, o)
    put_parts(jnp.concatenate([total, pieces], axis=1), outs)


def combine_grads_kernel(o_ref, back_ref, *outs):
    put_parts(dot(back_ref[...], o_ref[...]), outs)


def forward_kernel(x_ref, wg_ref, wu_ref, wd_ref, gate_ref, up_ref, hidden_ref, out_ref):
    x = x_ref[...]
    gate = dot(x, wg_ref[...])
    gate_ref[...] = gate
    gate_ref.send()
    up = dot(x, wu_ref[...])
    up_ref[...] = up
    up_ref.send()
    hidden = (gate * jax.nn.sigmoid(gate) * up).astype(BF16)
    hidden_ref[...] = hidden
    hidden_ref.send()
    for row in range(0, x_ref.shape[0], ROWS):
        here = slice(row, row + ROWS)
        out_ref[here] = dot(hidden[here], wd_ref[...]).astype(BF16)
        out_ref.send(here)


def backward_kernel(g_ref, wd_ref, gate_ref, up_ref, wg_ref, wu_ref, gg_ref, ug_ref, dx_ref):
    hidden_grad = dot_nt(g_ref[...], wd_ref[...])
    gate = gate_ref[...]
    squash = jax.nn.sigmoid(gate)
    gate_grad = hidden_grad * up_ref[...] * squash * (1.0 + gate * (1.0 - squash))
    gate_grad = gate_grad.astype(BF16)
    gg_ref[...] = gate_grad
    gg_ref.send()
    up_grad = (hidden_grad * gate * squash).astype(BF16)
    ug_ref[...] = up_grad
    ug_ref.send()
    for row in range(0, g_ref.shape[0], ROWS):
        here = slice(row, row + ROWS)
        part = dot_nt(gate_grad[here], wg_ref[...]) + dot_nt(up_grad[here], wu_ref[...])
        dx_ref[here] = part.astype(BF16)
        dx_ref.send(here)


def weight_grad_kernel(x_ref, pair_ref, hidden_ref, g_ref, *refs):
    received, (gu_ref, wd_ref) = refs[:-2], refs[-2:]
    f = hidden_ref.shape[1]
    for column in range(0, x_ref.shape[1], COLUMNS):
        here = slice(column, column + COLUMNS)
        v = dot_tn(x_ref[:, here], pair_ref[...])
        for i in range(2):
            one = v[:, i * f : (i + 1) * f]
            if received:
                one = one + received[0][i, here].astype(F32)
            gu_ref[i, here] = one.astype(BF16)
            gu_ref.send((i, here))
    v = dot_tn(hidden_ref[...], g_ref[...])
    if received:
        v = v + received[1][...].astype(F32)
    wd_ref[...] = v.astype(BF16)


def join_kernel(half, *refs):
    part_up, part_down, three_up, three_down, four_up, four_down, up_ref, down_ref = refs
    up_ref[:, :half] = (
        part_up[:, :half] + three_up[:, :half].astype(F32) + four_up[...].astype(F32)
    ).astype(BF16)
    up_ref[:, half:] = (part_up[:, half:] + three_up[:, half:].astype(F32)).astype(BF16)
    down_ref[:, :half] = (part_down[:, :half] + three_down[:, :half].astype(F32)).astype(BF16)
    down_ref[:, half:] = (
        part_down[:, half:] + three_down[:, half:].astype(F32) + four_down[...].astype(F32)
    ).astype(BF16)


def total_of(own, *others):
    total = own[...]
    for v in others:
        total = total + v[...].astype(F32)
    return total


def finish_out_kernel(*refs):
    out_ref, prob_ref = refs[-2:]
    total = total_of(*refs[:-2])
    d = out_ref.shape[1]
    out_ref[...] = total[:, :d].astype(BF16)
    pieces = total[:, d:].T
    prob_ref[...] = pieces[0:TOP] + (pieces[TOP : 2 * TOP] + pieces[2 * TOP : 3 * TOP])


def finish_grads_kernel(*refs):
    refs[-1][...] = total_of(*refs[:-1]).astype(BF16)


def nothing_kernel(first, second, out):
    pass


def cost(flops, args, out_shapes):
    nbytes = sum(a.size * a.dtype.itemsize for a in [*args, *out_shapes])
    return pl.CostEstimate(flops=flops, bytes_accessed=nbytes, transcendentals=0)


class Arriving:
    def __init__(self, ref, copies):
        self.ref, self.copies = ref, copies
        self.shape, self.dtype = ref.shape, ref.dtype

    def settle(self):
        for copy in self.copies:
            copy.wait()
        self.copies = []

    def __getitem__(self, at):
        self.settle()
        return self.ref[at]


class Leaving:
    def __init__(self, ref, target, next_sem):
        self.ref, self.target, self.next_sem, self.copies = ref, target, next_sem, []
        self.shape, self.dtype = ref.shape, ref.dtype

    def __setitem__(self, at, value):
        self.ref[at] = value

    def send(self, at=None):
        source, target = (self.ref, self.target) if at is None else (self.ref.at[at], self.target.at[at])
        copy = pltpu.make_async_copy(source, target, self.next_sem())
        copy.start()
        self.copies.append(copy)


MOST_SENDS = 16


def staged(kernel, scalars, near, read, unread, loads, made, *refs):
    first, rest = refs[: scalars + near], refs[scalars + near :]
    ins, rest = rest[:read], rest[read + unread :]
    outs, rest = rest[:made], rest[made:]
    held, rest = rest[: len(loads)], rest[len(loads) :]
    made_here, (in_sems, out_sems) = rest[:made], rest[made:]
    arriving, count = [], 0
    for here, (_, _, pieces) in zip(held, loads):
        copies = []
        for operand, source_at, target_at in pieces:
            source = ins[operand] if source_at is None else ins[operand].at[source_at]
            target = here if target_at is None else here.at[target_at]
            copies.append(pltpu.make_async_copy(source, target, in_sems.at[count]))
            copies[-1].start()
            count += 1
        arriving.append(Arriving(here, copies))
    sems = iter(range(MOST_SENDS))
    leaving = [Leaving(h, o, lambda: out_sems.at[next(sems)]) for h, o in zip(made_here, outs)]
    kernel(*first, *arriving, *leaving)
    for buffer in leaving:
        if not buffer.copies:
            buffer.send()
    for buffer in arriving:
        buffer.settle()
    for buffer in leaving:
        for copy in buffer.copies:
            copy.wait()


def call(kernel, out_shapes, args, scalars=0, near=0, unread=0, loads=None, flops=0, vmem=63):
    smem = pl.BlockSpec(memory_space=pltpu.SMEM)
    whole = pl.BlockSpec(memory_space=pltpu.VMEM)
    hbm = pl.BlockSpec(memory_space=pl.ANY)
    shapes = [jax.ShapeDtypeStruct(s, t) for s, t in out_shapes]
    read = len(args) - scalars - near - unread
    ins = args[scalars + near : scalars + near + read]
    if loads is None:
        loads = [(a.shape, a.dtype, [(i, None, None)]) for i, a in enumerate(ins)]
    copies = sum(len(pieces) for _, _, pieces in loads)
    counted = args[scalars : len(args) - unread] if flops else []
    return pl.pallas_call(
        functools.partial(staged, kernel, scalars, near, read, unread, loads, len(shapes)),
        out_shape=shapes,
        in_specs=[smem] * scalars + [whole] * near + [hbm] * (read + unread),
        out_specs=[hbm] * len(shapes),
        scratch_shapes=[pltpu.VMEM(shape, dtype) for shape, dtype, _ in loads]
        + [pltpu.VMEM(a.shape, a.dtype) for a in shapes]
        + [pltpu.SemaphoreType.DMA((copies,)), pltpu.SemaphoreType.DMA((MOST_SENDS,))],
        compiler_params=pltpu.CompilerParams(vmem_limit_bytes=vmem * MIB),
        cost_estimate=cost(flops, counted, shapes if flops else []),
    )(*args)


def small(kernel, out_shapes, args, vmem=8, flops=0):
    whole = pl.BlockSpec(memory_space=pltpu.VMEM)
    shapes = [jax.ShapeDtypeStruct(s, t) for s, t in out_shapes]
    return pl.pallas_call(
        kernel,
        out_shape=shapes,
        in_specs=[whole] * len(args),
        out_specs=[whole] * len(shapes),
        compiler_params=pltpu.CompilerParams(vmem_limit_bytes=vmem * MIB),
        cost_estimate=cost(flops, args, shapes),
    )(*args)


def beside(shape, one, other, at=None):
    width = shape[1]
    return (
        (shape[0], 2 * width),
        BF16,
        [
            (one, at, (slice(None), slice(0, width))),
            (other, at, (slice(None), slice(width, 2 * width))),
        ],
    )


def below(shape, one, other):
    height = shape[0]
    return (
        (2 * height, shape[1]),
        BF16,
        [(one, None, slice(0, height)), (other, None, slice(height, 2 * height))],
    )


def forward(x, gu, wd):
    rows, d = x.shape
    f = wd[0].shape[0]
    wide = (rows, 2 * f)
    return call(
        forward_kernel,
        [(wide, F32), (wide, F32), (wide, BF16), ((rows, d), BF16)],
        [x, *gu, *wd],
        loads=[
            (x.shape, BF16, [(0, None, None)]),
            beside((d, f), 1, 2, 0),
            beside((d, f), 1, 2, 1),
            below((f, d), 3, 4),
        ],
        flops=12 * rows * d * f,
    )


def backward(g, gate, up, gu, wd):
    rows, d = g.shape
    f = wd[0].shape[0]
    return call(
        backward_kernel,
        [((rows, 2 * f), BF16), ((rows, 2 * f), BF16), ((rows, d), BF16)],
        [g, gate, up, *gu, *wd],
        loads=[
            (g.shape, BF16, [(0, None, None)]),
            below((f, d), 5, 6),
            (gate.shape, F32, [(1, None, None)]),
            (up.shape, F32, [(2, None, None)]),
            beside((d, f), 3, 4, 0),
            beside((d, f), 3, 4, 1),
        ],
        flops=12 * rows * d * f,
    )


def weight_grads(x, g, gg, ug, hidden, half, received=()):
    rows, d = x.shape
    f = gg.shape[1] // 2
    mine = (slice(None), slice(half * f, (half + 1) * f))
    pair = [(2, mine, (slice(None), slice(0, f))), (3, mine, (slice(None), slice(f, 2 * f)))]
    return call(
        weight_grad_kernel,
        [((2, d, f), BF16), ((f, d), BF16)],
        [x, g, gg, ug, hidden, *received],
        loads=[
            (x.shape, BF16, [(0, None, None)]),
            ((rows, 2 * f), BF16, pair),
            ((rows, f), BF16, [(4, mine, None)]),
            (g.shape, BF16, [(1, None, None)]),
        ]
        + [(v.shape, BF16, [(5 + i, None, None)]) for i, v in enumerate(received)],
        flops=0 if received else 6 * rows * d * f,
    )


def after(value, earlier):
    hbm = pl.BlockSpec(memory_space=pl.ANY)
    return pl.pallas_call(
        nothing_kernel,
        out_shape=jax.ShapeDtypeStruct(value.shape, value.dtype),
        in_specs=[hbm, hbm],
        out_specs=hbm,
        input_output_aliases={0: 0},
        cost_estimate=pl.CostEstimate(flops=0, bytes_accessed=0, transcendentals=0),
    )(value, earlier)


ORDER = (0, -1, 1, -2, 2, -3, 3, 4)


def shift_z(v, step):
    return lax.ppermute(v, "z", [(i, (i + step) % NZ) for i in range(NZ)])


def gather_z(own):
    held = {0: own}
    for hop in range(1, 5):
        if hop < 4:
            held[-hop] = shift_z(held[1 - hop], 1)
        held[hop] = shift_z(held[hop - 1], -1)
    return [held[r] for r in ORDER]


def part_shapes(t, width):
    half = (width // 2 + 127) // 128 * 128
    kinds = [F32 if r in (0, -2, 2) else BF16 for r in ORDER[:-1]]
    return [((t, width), k) for k in kinds] + [((t, half), BF16), ((t, width - half), BF16)]


def scatter_z(parts, finish, out_shapes):
    part = dict(zip(ORDER[:-1], parts))
    far_up, far_down = parts[NZ - 1 :]
    three_up, three_down = shift_z(part[3], 1), shift_z(part[-3], -1)
    four_up, four_down = shift_z(far_up, 2), shift_z(far_down, -2)
    one_up, one_down = shift_z(part[1], 1), shift_z(part[-1], -1)
    two_up, two_down = small(
        functools.partial(join_kernel, far_up.shape[1]),
        [(part[2].shape, BF16)] * 2,
        [part[2], part[-2], three_up, three_down, four_up, four_down],
    )
    two_up, two_down = shift_z(two_up, 2), shift_z(two_down, -2)
    return small(finish, out_shapes, [part[0], one_up, one_down, two_up, two_down])


def swap_dp(v):
    return lax.ppermute(v, "dp", [(0, 1), (1, 0)])


def exchange_plane(rows):
    r, d = rows.shape
    out = lax.all_to_all(
        rows.reshape(PLANE, r // PLANE, d), ("x", "y"), split_axis=0, concat_axis=0, tiled=True
    )
    return out.reshape(r, d)


def on_device(tokens, expert_ids, route_weight, w_gate_up, w_down, out_grad):
    t, d = tokens.shape[1:]
    n = t * NZ
    rows = PLANE * NZ * SLOTS
    z = lax.axis_index("z").astype(jnp.int32).reshape(1)

    gu = (w_gate_up[0], swap_dp(w_gate_up[0]))
    wd = (w_down[0], swap_dp(w_down[0]))
    (blob,) = small(
        blob_kernel, [((t, d + 128), BF16)], [expert_ids[0].T, route_weight[0].T, tokens[0]]
    )
    blobs = gather_z(blob)
    send_x, placing, row_weight, ids = call(
        place_tokens_kernel,
        [((rows, d), BF16), ((rows, n), BF16), ((rows, 128), F32), ((TOP, n), F32)],
        [z, *blobs, gu[1], wd[1]],
        scalars=1,
        near=NZ,
        unread=2,
        vmem=62,
        flops=2 * rows * n * d,
    )
    x = exchange_plane(send_x)
    grads = gather_z(out_grad[0])
    send_g, back, flat = call(
        place_grads_kernel,
        [((rows, d), BF16), ((n, rows), BF16), ((TOP, rows), F32)],
        [*grads, placing, row_weight],
        near=NZ,
        flops=2 * rows * n * d,
        vmem=62,
    )
    g = exchange_plane(send_g)
    gate, up, hidden, out_rows = forward(x, gu, wd)
    o = exchange_plane(after(out_rows, g))
    gate_grad, up_grad, grad_rows = backward(g, gate, up, gu, wd)
    grad_rows = after(grad_rows, o)
    dx = exchange_plane(grad_rows)

    away = weight_grads(x, g, gate_grad, up_grad, hidden, 1)
    received = [swap_dp(v) for v in away]
    grad_gate_up, grad_down = weight_grads(x, g, gate_grad, up_grad, hidden, 0, received)

    parts = call(
        combine_out_kernel,
        part_shapes(t, d + 128),
        [z, o, send_g, placing, back, row_weight, flat, ids, away[0], grad_rows],
        scalars=1,
        unread=2,
    )
    layer_out, prob_grad = scatter_z(
        parts, finish_out_kernel, [((t, d), BF16), ((TOP, t), F32)]
    )
    dx = after(dx, grad_gate_up)
    parts = small(
        combine_grads_kernel,
        part_shapes(t, d),
        [dx, back],
        vmem=48,
        flops=2 * rows * n * d,
    )
    (token_grad,) = scatter_z(parts, finish_grads_kernel, [((t, d), BF16)])
    return (
        layer_out[None],
        token_grad[None],
        prob_grad.T[None],
        grad_gate_up[None],
        grad_down[None],
    )


def solution(mesh):
    fine = Mesh(mesh.devices.reshape(NX, NY, NZ, 2), ("x", "y", "z", "dp"))
    expert = ("x", "y", "z")
    by_token = P("dp", expert, None)
    specs = (by_token, by_token, by_token, P(expert, None, None, "dp"), P(expert, "dp", None))
    return jax.shard_map(
        on_device,
        mesh=fine,
        in_specs=specs + (by_token,),
        out_specs=(by_token, by_token, by_token, specs[3], specs[4]),
        check_vma=False,
    )
```

```python
import functools

import jax
import jax.numpy as jnp
import numpy as np
from jax import lax
from jax.experimental import pallas as pl
from jax.experimental.pallas import tpu as pltpu
from jax.sharding import Mesh, PartitionSpec as P

F32 = jnp.float32
BF16 = jnp.bfloat16
NX, NY, NZ = 4, 4, 8
PLANE = NX * NY
SLOTS = 4
TOP = 8
MIB = 1 << 20
ROWS = 256
COLUMNS = 1024


def dot(a, b):
    return jnp.dot(a, b, preferred_element_type=F32)


def dot_nt(a, b):
    return lax.dot_general(a, b, (((1,), (1,)), ((), ())), preferred_element_type=F32)


def dot_tn(a, b):
    return lax.dot_general(a, b, (((0,), (0,)), ((), ())), preferred_element_type=F32)


def split3(v):
    hi = v.astype(BF16)
    rest = v - hi.astype(F32)
    mid = rest.astype(BF16)
    lo = (rest - mid.astype(F32)).astype(BF16)
    return hi, mid, lo


ORDER = (0, -1, 1, -2, 2, -3, 3, 4)


def place(meta, z):
    n = meta.shape[0]
    rows = PLANE * NZ * SLOTS
    turned = meta.T
    ids = turned[0:TOP]
    weights = turned[TOP : 2 * TOP] + turned[2 * TOP : 3 * TOP] + turned[3 * TOP : 4 * TOP]
    expert = (lax.broadcasted_iota(jnp.int32, (PLANE, n), 0) * NZ + z).astype(F32)
    named = jnp.zeros((PLANE, n), F32)
    weight = jnp.zeros((PLANE, n), F32)
    for k in range(TOP):
        hit = ids[k : k + 1] == expert
        named = jnp.where(hit, 1.0, named)
        weight = jnp.where(hit, weights[k : k + 1], weight)
    block = n // NZ
    shift = block.bit_length() - 1
    from_t = lax.broadcasted_iota(jnp.int32, (n, n), 0)
    to_t = lax.broadcasted_iota(jnp.int32, (n, n), 1)
    same = lax.shift_right_logical(from_t, shift) == lax.shift_right_logical(to_t, shift)
    before = jnp.where(same & (from_t < to_t), 1.0, 0.0).astype(BF16)
    rank = dot(named.astype(BF16), before)
    rank = jnp.where(named > 0.5, rank, -1.0)

    def spread(v):
        return jnp.broadcast_to(v[:, None, :], (PLANE, NZ * SLOTS, n)).reshape(rows, n)

    row = lax.broadcasted_iota(jnp.int32, (rows, n), 0)
    col = lax.broadcasted_iota(jnp.int32, (rows, n), 1)
    row_block = lax.shift_right_logical(row, 2) & (NZ - 1)
    slot = (row & (SLOTS - 1)).astype(F32)
    here = (spread(rank) == slot) & (lax.shift_right_logical(col, shift) == row_block)
    placing = jnp.where(here, 1.0, 0.0)
    row_weight = jnp.sum(jnp.where(here, spread(weight), 0.0), axis=1, keepdims=True)
    return placing, row_weight, ids


def blob_kernel(ids_ref, weight_ref, tokens_ref, blob_ref):
    t, d = tokens_ref.shape
    pieces = [v.astype(F32) for v in split3(weight_ref[...])]
    rest = jnp.zeros((128 - 4 * TOP, t), F32)
    meta = jnp.concatenate([ids_ref[...].astype(F32), *pieces, rest], axis=0)
    blob_ref[:, :d] = tokens_ref[...]
    blob_ref[:, d:] = meta.T.astype(BF16)


def place_tokens_kernel(z_ref, *refs):
    blobs, (x_ref, placing_ref, weight_ref, ids_ref) = refs[:NZ], refs[NZ:]
    d = x_ref.shape[1]
    meta = jnp.concatenate([b[:, d:].astype(F32) for b in blobs], axis=0)
    placing, row_weight, ids = place(meta, z_ref[0])
    placing = placing.astype(BF16)
    placing_ref[...] = placing
    weight_ref[...] = jnp.broadcast_to(row_weight, weight_ref.shape)
    ids_ref[...] = ids
    tokens = jnp.concatenate([b[:, :d] for b in blobs], axis=0)
    for row in range(0, x_ref.shape[0], ROWS):
        here = slice(row, row + ROWS)
        x_ref[here] = dot(placing[here], tokens).astype(BF16)
        x_ref.send(here)


def place_grads_kernel(*refs):
    grads, (placing_ref, weight_ref, g_ref) = refs[:NZ], refs[NZ:]
    placing = placing_ref[...]
    og = jnp.concatenate([b[...] for b in grads], axis=0)
    for row in range(0, g_ref.shape[0], ROWS):
        here = slice(row, row + ROWS)
        g_ref[here] = (dot(placing[here], og) * weight_ref[here, 0:1]).astype(BF16)
        g_ref.send(here)


def put_parts(total, outs):
    block = total.shape[0] // NZ
    part = {r: total[i * block : (i + 1) * block] for i, r in enumerate(ORDER)}
    own, two_up, two_down, up, down, *far = outs
    own[...] = part[0]
    two_up[...] = part[2]
    two_down[...] = part[-2]
    for out, sign in ((up, 1), (down, -1)):
        out[:block] = part[3 * sign].astype(BF16)
        out[block:] = part[sign].astype(BF16)
    last, at = part[4].astype(BF16), 0
    for out in far:
        out[...] = last[:, at : at + out.shape[1]]
        at += out.shape[1]


def combine_out_kernel(
    z_ref, placing_ref, weight_ref, ids_ref, o_ref, g_ref, back_ref, *outs
):
    rows = o_ref.shape[0]
    placing = placing_ref[...].astype(F32)
    n = placing.shape[1]
    row_weight = weight_ref[:, 0:1]
    back_ref[...] = placing.T.astype(BF16)
    back_ref.send()
    weighted = (placing * row_weight).T
    hi = weighted.astype(BF16)
    lo = (weighted - hi.astype(F32)).astype(BF16)
    o = o_ref[...]
    inverse = jnp.where(row_weight > 0.0, 1.0 / jnp.where(row_weight > 0.0, row_weight, 1.0), 0.0)
    dots = jnp.sum(g_ref[...].astype(F32) * o.astype(F32), axis=1, keepdims=True) * inverse
    per_expert = jnp.sum(
        (placing * dots).reshape(PLANE, rows // PLANE, n), axis=1
    )
    expert = (lax.broadcasted_iota(jnp.int32, (PLANE, n), 0) * NZ + z_ref[0]).astype(F32)
    ids = ids_ref[...]
    probs = jnp.concatenate(
        [
            jnp.sum(jnp.where(ids[k : k + 1] == expert, per_expert, 0.0), axis=0, keepdims=True)
            for k in range(TOP)
        ],
        axis=0,
    )
    pieces = [v.astype(F32) for v in split3(probs)]
    pieces = jnp.concatenate([*pieces, jnp.zeros((128 - 3 * TOP, n), F32)], axis=0).T
    total = dot(hi, o) + dot(lo, o)
    put_parts(jnp.concatenate([total, pieces], axis=1), outs)


def combine_grads_kernel(o_ref, back_ref, *outs):
    put_parts(dot(back_ref[...], o_ref[...]), outs)


def forward_kernel(x_ref, wg_ref, wu_ref, wd_ref, slope_ref, swish_ref, hidden_ref, out_ref):
    x = x_ref[...]
    gate = dot(x, wg_ref[...])
    up = dot(x, wu_ref[...])
    squash = jax.nn.sigmoid(gate)
    swish = gate * squash
    hidden = (swish * up).astype(BF16)
    hidden_ref[...] = hidden
    hidden_ref.send()
    swish_ref[...] = swish
    swish_ref.send()
    slope_ref[...] = up * squash * (1.0 + gate * (1.0 - squash))
    slope_ref.send()
    for row in range(0, x_ref.shape[0], ROWS):
        here = slice(row, row + ROWS)
        out_ref[here] = dot(hidden[here], wd_ref[...]).astype(BF16)
        out_ref.send(here)


def backward_kernel(g_ref, wd_ref, slope_ref, swish_ref, wg_ref, wu_ref, gg_ref, ug_ref, dx_ref):
    hidden_grad = dot_nt(g_ref[...], wd_ref[...])
    gate_grad = (hidden_grad * slope_ref[...]).astype(BF16)
    gg_ref[...] = gate_grad
    gg_ref.send()
    up_grad = (hidden_grad * swish_ref[...]).astype(BF16)
    ug_ref[...] = up_grad
    ug_ref.send()
    for row in range(0, g_ref.shape[0], ROWS):
        here = slice(row, row + ROWS)
        part = dot_nt(gate_grad[here], wg_ref[...]) + dot_nt(up_grad[here], wu_ref[...])
        dx_ref[here] = part.astype(BF16)
        dx_ref.send(here)


def weight_grad_kernel(x_ref, pair_ref, hidden_ref, g_ref, *refs):
    received, (gu_ref, wd_ref) = refs[:-2], refs[-2:]
    f = hidden_ref.shape[1]
    for column in range(0, x_ref.shape[1], COLUMNS):
        here = slice(column, column + COLUMNS)
        v = dot_tn(x_ref[:, here], pair_ref[...])
        for i in range(2):
            one = v[:, i * f : (i + 1) * f]
            if received:
                one = one + received[0][i, here].astype(F32)
            gu_ref[i, here] = one.astype(BF16)
            gu_ref.send((i, here))
    v = dot_tn(hidden_ref[...], g_ref[...])
    if received:
        v = v + received[1][...].astype(F32)
    wd_ref[...] = v.astype(BF16)


def join_kernel(part_up, part_down, from_below, from_above, *refs):
    far, (up_ref, down_ref) = refs[:-2], refs[-2:]
    block = part_up.shape[0]
    up = part_up[...] + from_below[:block].astype(F32)
    down = part_down[...] + from_above[:block].astype(F32)
    half = far[0].shape[1]
    up_ref[:, :half] = (up[:, :half] + far[0][...].astype(F32)).astype(BF16)
    if len(far) == 1:
        down_ref[...] = down.astype(BF16)
    else:
        up_ref[:, half:] = up[:, half:].astype(BF16)
        down_ref[:, :half] = down[:, :half].astype(BF16)
        down_ref[:, half:] = (down[:, half:] + far[1][...].astype(F32)).astype(BF16)


def total_of(own, from_below, from_above, two_below, two_above):
    block = own.shape[0]
    total = own[...] + (from_below[block:].astype(F32) + from_above[block:].astype(F32))
    return total + (two_below[...].astype(F32) + two_above[...].astype(F32))


def finish_out_kernel(*refs):
    out_ref, prob_ref = refs[-2:]
    total = total_of(*refs[:-2])
    d = out_ref.shape[1]
    out_ref[...] = total[:, :d].astype(BF16)
    pieces = total[:, d:].T
    prob_ref[...] = pieces[0:TOP] + (pieces[TOP : 2 * TOP] + pieces[2 * TOP : 3 * TOP])


def finish_grads_kernel(*refs):
    refs[-1][...] = total_of(*refs[:-1]).astype(BF16)


def nothing_kernel(first, second, out):
    pass


def cost(flops, args, out_shapes):
    nbytes = sum(a.size * a.dtype.itemsize for a in [*args, *out_shapes])
    return pl.CostEstimate(flops=flops, bytes_accessed=nbytes, transcendentals=0)


class Arriving:
    def __init__(self, ref, copies):
        self.ref, self.copies, self.later = ref, copies, []
        self.shape, self.dtype = ref.shape, ref.dtype

    def start(self):
        for copy in self.copies:
            copy.start()

    def settle(self):
        for copy in self.copies:
            copy.wait()
        for buffer in self.later:
            buffer.start()
        self.copies, self.later = [], []

    def __getitem__(self, at):
        self.settle()
        return self.ref[at]


class Leaving:
    def __init__(self, ref, target, next_sem):
        self.ref, self.target, self.next_sem, self.copies = ref, target, next_sem, []
        self.shape, self.dtype = ref.shape, ref.dtype

    def __setitem__(self, at, value):
        self.ref[at] = value

    def send(self, at=None):
        source, target = (self.ref, self.target) if at is None else (self.ref.at[at], self.target.at[at])
        copy = pltpu.make_async_copy(source, target, self.next_sem())
        copy.start()
        self.copies.append(copy)


MOST_SENDS = 16


def staged(kernel, scalars, near, read, unread, loads, eager, made, *refs):
    first, rest = refs[: scalars + near], refs[scalars + near :]
    ins, rest = rest[:read], rest[read + unread :]
    outs, rest = rest[:made], rest[made:]
    held, rest = rest[: len(loads)], rest[len(loads) :]
    made_here, (in_sems, out_sems) = rest[:made], rest[made:]
    arriving, count = [], 0
    for here, (_, _, pieces) in zip(held, loads):
        copies = []
        for operand, source_at, target_at in pieces:
            source = ins[operand] if source_at is None else ins[operand].at[source_at]
            target = here if target_at is None else here.at[target_at]
            copies.append(pltpu.make_async_copy(source, target, in_sems.at[count]))
            count += 1
        arriving.append(Arriving(here, copies))
    for buffer in arriving[:eager]:
        buffer.start()
    if arriving[eager:]:
        arriving[eager - 1].later = arriving[eager:]
    sems = iter(range(MOST_SENDS))
    leaving = [Leaving(h, o, lambda: out_sems.at[next(sems)]) for h, o in zip(made_here, outs)]
    kernel(*first, *arriving, *leaving)
    for buffer in leaving:
        if not buffer.copies:
            buffer.send()
    for buffer in arriving:
        buffer.settle()
    for buffer in leaving:
        for copy in buffer.copies:
            copy.wait()


def call(
    kernel, out_shapes, args, scalars=0, near=0, unread=0, loads=None, eager=99, flops=0, vmem=63
):
    smem = pl.BlockSpec(memory_space=pltpu.SMEM)
    whole = pl.BlockSpec(memory_space=pltpu.VMEM)
    hbm = pl.BlockSpec(memory_space=pl.ANY)
    shapes = [jax.ShapeDtypeStruct(s, t) for s, t in out_shapes]
    read = len(args) - scalars - near - unread
    ins = args[scalars + near : scalars + near + read]
    if loads is None:
        loads = [(a.shape, a.dtype, [(i, None, None)]) for i, a in enumerate(ins)]
    copies = sum(len(pieces) for _, _, pieces in loads)
    counted = args[scalars : len(args) - unread] if flops else []
    return pl.pallas_call(
        functools.partial(
            staged, kernel, scalars, near, read, unread, loads, eager, len(shapes)
        ),
        out_shape=shapes,
        in_specs=[smem] * scalars + [whole] * near + [hbm] * (read + unread),
        out_specs=[hbm] * len(shapes),
        scratch_shapes=[pltpu.VMEM(shape, dtype) for shape, dtype, _ in loads]
        + [pltpu.VMEM(a.shape, a.dtype) for a in shapes]
        + [pltpu.SemaphoreType.DMA((copies,)), pltpu.SemaphoreType.DMA((MOST_SENDS,))],
        compiler_params=pltpu.CompilerParams(vmem_limit_bytes=vmem * MIB),
        cost_estimate=cost(flops, counted, shapes if flops else []),
    )(*args)


def dropping(kernel, read, unread, *refs):
    kernel(*refs[:read], *refs[read + unread :])


def small(kernel, out_shapes, args, unread=0, vmem=8, flops=0):
    whole = pl.BlockSpec(memory_space=pltpu.VMEM)
    hbm = pl.BlockSpec(memory_space=pl.ANY)
    shapes = [jax.ShapeDtypeStruct(s, t) for s, t in out_shapes]
    read = len(args) - unread
    return pl.pallas_call(
        functools.partial(dropping, kernel, read, unread),
        out_shape=shapes,
        in_specs=[whole] * read + [hbm] * unread,
        out_specs=[whole] * len(shapes),
        compiler_params=pltpu.CompilerParams(vmem_limit_bytes=vmem * MIB),
        cost_estimate=cost(flops, args[:read], shapes),
    )(*args)


def beside(shape, one, other, at=None):
    width = shape[1]
    return (
        (shape[0], 2 * width),
        BF16,
        [
            (one, at, (slice(None), slice(0, width))),
            (other, at, (slice(None), slice(width, 2 * width))),
        ],
    )


def below(shape, one, other):
    height = shape[0]
    return (
        (2 * height, shape[1]),
        BF16,
        [(one, None, slice(0, height)), (other, None, slice(height, 2 * height))],
    )


def forward(x, gu, wd):
    rows, d = x.shape
    f = wd[0].shape[0]
    wide = (rows, 2 * f)
    return call(
        forward_kernel,
        [(wide, F32), (wide, F32), (wide, BF16), ((rows, d), BF16)],
        [x, *gu, *wd],
        loads=[
            (x.shape, BF16, [(0, None, None)]),
            beside((d, f), 1, 2, 0),
            beside((d, f), 1, 2, 1),
            below((f, d), 3, 4),
        ],
        eager=2,
        flops=12 * rows * d * f,
    )


def backward(g, slope, swish, gu, wd):
    rows, d = g.shape
    f = wd[0].shape[0]
    return call(
        backward_kernel,
        [((rows, 2 * f), BF16), ((rows, 2 * f), BF16), ((rows, d), BF16)],
        [g, slope, swish, *gu, *wd],
        loads=[
            (g.shape, BF16, [(0, None, None)]),
            below((f, d), 5, 6),
            (slope.shape, F32, [(1, None, None)]),
            (swish.shape, F32, [(2, None, None)]),
            beside((d, f), 3, 4, 0),
            beside((d, f), 3, 4, 1),
        ],
        eager=2,
        flops=12 * rows * d * f,
    )


def weight_grads(x, g, gg, ug, hidden, half, received=()):
    rows, d = x.shape
    f = gg.shape[1] // 2
    mine = (slice(None), slice(half * f, (half + 1) * f))
    pair = [(2, mine, (slice(None), slice(0, f))), (3, mine, (slice(None), slice(f, 2 * f)))]
    return call(
        weight_grad_kernel,
        [((2, d, f), BF16), ((f, d), BF16)],
        [x, g, gg, ug, hidden, *received],
        loads=[
            (x.shape, BF16, [(0, None, None)]),
            ((rows, 2 * f), BF16, pair),
            ((rows, f), BF16, [(4, mine, None)]),
            (g.shape, BF16, [(1, None, None)]),
        ]
        + [(v.shape, BF16, [(5 + i, None, None)]) for i, v in enumerate(received)],
        eager=2,
        flops=0 if received else 6 * rows * d * f,
    )


def after(value, earlier):
    hbm = pl.BlockSpec(memory_space=pl.ANY)
    return pl.pallas_call(
        nothing_kernel,
        out_shape=jax.ShapeDtypeStruct(value.shape, value.dtype),
        in_specs=[hbm, hbm],
        out_specs=hbm,
        input_output_aliases={0: 0},
        cost_estimate=pl.CostEstimate(flops=0, bytes_accessed=0, transcendentals=0),
    )(value, earlier)


def shift_z(v, step):
    return lax.ppermute(v, "z", [(i, (i + step) % NZ) for i in range(NZ)])


def first_hop(own):
    return shift_z(own, 1), shift_z(own, -1)


def gather_z(own, first):
    held = {0: own, -1: first[0], 1: first[1]}
    for hop in range(2, 5):
        if hop < 4:
            held[-hop] = shift_z(held[1 - hop], 1)
        held[hop] = shift_z(held[hop - 1], -1)
    return [held[r] for r in ORDER]


def part_shapes(t, width, pieces):
    return [((t, width), F32)] * 3 + [((2 * t, width), BF16)] * 2 + [((t, width // pieces), BF16)] * pieces


def scatter_z(parts, finish, out_shapes, earlier=()):
    own, two_up, two_down, up, down, *far = parts
    from_below, from_above = shift_z(up, 1), shift_z(down, -1)
    far = [shift_z(v, step) for v, step in zip(far, (2, -2))]
    two_up, two_down = small(
        join_kernel,
        [(two_up.shape, BF16)] * 2,
        [two_up, two_down, from_below, from_above, *far, *earlier],
        unread=len(earlier),
    )
    two_below, two_above = shift_z(two_up, 2), shift_z(two_down, -2)
    return small(finish, out_shapes, [own, from_below, from_above, two_below, two_above])


def swap_dp(v):
    return lax.ppermute(v, "dp", [(0, 1), (1, 0)])


def exchange_plane(rows):
    r, d = rows.shape
    out = lax.all_to_all(
        rows.reshape(PLANE, r // PLANE, d), ("x", "y"), split_axis=0, concat_axis=0, tiled=True
    )
    return out.reshape(r, d)


def on_device(tokens, expert_ids, route_weight, w_gate_up, w_down, out_grad):
    t, d = tokens.shape[1:]
    n = t * NZ
    rows = PLANE * NZ * SLOTS
    z = lax.axis_index("z").astype(jnp.int32).reshape(1)

    gu = (w_gate_up[0], swap_dp(w_gate_up[0]))
    wd = (w_down[0], swap_dp(w_down[0]))
    (blob,) = call(
        blob_kernel, [((t, d + 128), BF16)], [expert_ids[0].T, route_weight[0].T, tokens[0]]
    )
    blobs = gather_z(blob, first_hop(blob))
    first = first_hop(out_grad[0])
    send_x, placing, row_weight, ids = call(
        place_tokens_kernel,
        [((rows, d), BF16), ((rows, n), BF16), ((rows, 128), F32), ((TOP, n), F32)],
        [z, *blobs, gu[1], wd[1], *first],
        scalars=1,
        near=NZ,
        unread=4,
        vmem=62,
        flops=2 * rows * n * d,
    )
    x = exchange_plane(send_x)
    grads = gather_z(out_grad[0], first)
    (send_g,) = call(
        place_grads_kernel,
        [((rows, d), BF16)],
        [*grads, placing, row_weight],
        near=NZ,
        flops=2 * rows * n * d,
        vmem=62,
    )
    g = exchange_plane(send_g)
    slope, swish, hidden, out_rows = forward(x, gu, wd)
    o = exchange_plane(after(out_rows, g))
    gate_grad, up_grad, grad_rows = backward(g, slope, swish, gu, wd)
    grad_rows = after(grad_rows, o)
    dx = exchange_plane(grad_rows)

    away = weight_grads(x, g, gate_grad, up_grad, hidden, 1)
    received = [swap_dp(v) for v in away]
    grad_gate_up, grad_down = weight_grads(x, g, gate_grad, up_grad, hidden, 0, received)

    back, *parts = call(
        combine_out_kernel,
        [((n, rows), BF16)] + part_shapes(t, d + 128, 1),
        [z, placing, row_weight, ids, o, send_g, away[0], grad_rows],
        scalars=1,
        unread=2,
    )
    layer_out, prob_grad = scatter_z(
        parts, finish_out_kernel, [((t, d), BF16), ((TOP, t), F32)], [grad_gate_up]
    )
    parts = small(
        combine_grads_kernel,
        part_shapes(t, d, 2),
        [after(dx, layer_out), back],
        vmem=48,
        flops=2 * rows * n * d,
    )
    (token_grad,) = scatter_z(parts, finish_grads_kernel, [((t, d), BF16)])
    return (
        layer_out[None],
        token_grad[None],
        prob_grad.T[None],
        grad_gate_up[None],
        grad_down[None],
    )


def solution(mesh):
    fine = Mesh(mesh.devices.reshape(NX, NY, NZ, 2), ("x", "y", "z", "dp"))
    expert = ("x", "y", "z")
    by_token = P("dp", expert, None)
    specs = (by_token, by_token, by_token, P(expert, None, None, "dp"), P(expert, "dp", None))
    return jax.shard_map(
        on_device,
        mesh=fine,
        in_specs=specs + (by_token,),
        out_specs=(by_token, by_token, by_token, specs[3], specs[4]),
        check_vma=False,
    )
```

```python
import functools

import jax
import jax.numpy as jnp
import numpy as np
from jax import lax
from jax.experimental import pallas as pl
from jax.experimental.pallas import tpu as pltpu
from jax.sharding import Mesh, PartitionSpec as P

F32 = jnp.float32
BF16 = jnp.bfloat16
NX, NY, NZ = 4, 4, 8
PLANE = NX * NY
SLOTS = 4
TOP = 8
MIB = 1 << 20
ROWS = 256
COLUMNS = 1024


def dot(a, b):
    return jnp.dot(a, b, preferred_element_type=F32)


def dot_nt(a, b):
    return lax.dot_general(a, b, (((1,), (1,)), ((), ())), preferred_element_type=F32)


def dot_tn(a, b):
    return lax.dot_general(a, b, (((0,), (0,)), ((), ())), preferred_element_type=F32)


def split3(v):
    hi = v.astype(BF16)
    rest = v - hi.astype(F32)
    mid = rest.astype(BF16)
    lo = (rest - mid.astype(F32)).astype(BF16)
    return hi, mid, lo


ORDER = (0, -1, 1, -2, 2, -3, 3, 4)


def place(meta, z):
    n = meta.shape[0]
    rows = PLANE * NZ * SLOTS
    turned = meta.T
    ids = turned[0:TOP]
    weights = turned[TOP : 2 * TOP] + turned[2 * TOP : 3 * TOP] + turned[3 * TOP : 4 * TOP]
    expert = (lax.broadcasted_iota(jnp.int32, (PLANE, n), 0) * NZ + z).astype(F32)
    named = jnp.zeros((PLANE, n), F32)
    weight = jnp.zeros((PLANE, n), F32)
    for k in range(TOP):
        hit = ids[k : k + 1] == expert
        named = jnp.where(hit, 1.0, named)
        weight = jnp.where(hit, weights[k : k + 1], weight)
    block = n // NZ
    shift = block.bit_length() - 1
    from_t = lax.broadcasted_iota(jnp.int32, (n, n), 0)
    to_t = lax.broadcasted_iota(jnp.int32, (n, n), 1)
    same = lax.shift_right_logical(from_t, shift) == lax.shift_right_logical(to_t, shift)
    before = jnp.where(same & (from_t < to_t), 1.0, 0.0).astype(BF16)
    rank = dot(named.astype(BF16), before)
    rank = jnp.where(named > 0.5, rank, -1.0)

    def spread(v):
        return jnp.broadcast_to(v[:, None, :], (PLANE, NZ * SLOTS, n)).reshape(rows, n)

    row = lax.broadcasted_iota(jnp.int32, (rows, n), 0)
    col = lax.broadcasted_iota(jnp.int32, (rows, n), 1)
    row_block = lax.shift_right_logical(row, 2) & (NZ - 1)
    slot = (row & (SLOTS - 1)).astype(F32)
    here = (spread(rank) == slot) & (lax.shift_right_logical(col, shift) == row_block)
    placing = jnp.where(here, 1.0, 0.0)
    row_weight = jnp.sum(jnp.where(here, spread(weight), 0.0), axis=1, keepdims=True)
    return placing, row_weight, ids


def blob_kernel(ids_ref, weight_ref, tokens_ref, blob_ref):
    t, d = tokens_ref.shape
    pieces = [v.astype(F32) for v in split3(weight_ref[...])]
    rest = jnp.zeros((128 - 4 * TOP, t), F32)
    meta = jnp.concatenate([ids_ref[...].astype(F32), *pieces, rest], axis=0)
    blob_ref[:, :d] = tokens_ref[...]
    blob_ref[:, d:] = meta.T.astype(BF16)


def place_tokens_kernel(z_ref, *refs):
    blobs, (x_ref, placing_ref, weight_ref, ids_ref) = refs[:NZ], refs[NZ:]
    d = x_ref.shape[1]
    meta = jnp.concatenate([b[:, d:].astype(F32) for b in blobs], axis=0)
    placing, row_weight, ids = place(meta, z_ref[0])
    placing = placing.astype(BF16)
    placing_ref[...] = placing
    weight_ref[...] = jnp.broadcast_to(row_weight, weight_ref.shape)
    ids_ref[...] = ids
    tokens = jnp.concatenate([b[:, :d] for b in blobs], axis=0)
    for row in range(0, x_ref.shape[0], ROWS):
        here = slice(row, row + ROWS)
        x_ref[here] = dot(placing[here], tokens).astype(BF16)
        x_ref.send(here)


def place_grads_kernel(*refs):
    grads, (placing_ref, weight_ref, g_ref) = refs[:NZ], refs[NZ:]
    placing = placing_ref[...]
    og = jnp.concatenate([b[...] for b in grads], axis=0)
    for row in range(0, g_ref.shape[0], ROWS):
        here = slice(row, row + ROWS)
        g_ref[here] = (dot(placing[here], og) * weight_ref[here, 0:1]).astype(BF16)
        g_ref.send(here)


def put_parts(total, outs):
    block = total.shape[0] // NZ
    part = {r: total[i * block : (i + 1) * block] for i, r in enumerate(ORDER)}
    own, two_up, two_down, up, down, *far = outs
    half = far[0].shape[1]
    own[...] = part[0]
    two_up[...] = part[2]
    two_down[...] = part[-2]
    for out, sign in ((up, 1), (down, -1)):
        out[:block] = part[3 * sign].astype(BF16)
        out[block:] = part[sign].astype(BF16)
    last = part[4].astype(BF16)
    far[0][...] = last[:, :half]
    far[1][...] = last[:, half:]


def combine_out_kernel(
    z_ref, placing_ref, weight_ref, ids_ref, o_ref, g_ref, back_ref, *outs
):
    rows = o_ref.shape[0]
    placing = placing_ref[...].astype(F32)
    n = placing.shape[1]
    row_weight = weight_ref[:, 0:1]
    back_ref[...] = placing.T.astype(BF16)
    back_ref.send()
    weighted = (placing * row_weight).T
    hi = weighted.astype(BF16)
    lo = (weighted - hi.astype(F32)).astype(BF16)
    o = o_ref[...]
    inverse = jnp.where(row_weight > 0.0, 1.0 / jnp.where(row_weight > 0.0, row_weight, 1.0), 0.0)
    dots = jnp.sum(g_ref[...].astype(F32) * o.astype(F32), axis=1, keepdims=True) * inverse
    per_expert = jnp.sum(
        (placing * dots).reshape(PLANE, rows // PLANE, n), axis=1
    )
    expert = (lax.broadcasted_iota(jnp.int32, (PLANE, n), 0) * NZ + z_ref[0]).astype(F32)
    ids = ids_ref[...]
    probs = jnp.concatenate(
        [
            jnp.sum(jnp.where(ids[k : k + 1] == expert, per_expert, 0.0), axis=0, keepdims=True)
            for k in range(TOP)
        ],
        axis=0,
    )
    pieces = [v.astype(F32) for v in split3(probs)]
    pieces = jnp.concatenate([*pieces, jnp.zeros((128 - 3 * TOP, n), F32)], axis=0).T
    total = dot(hi, o) + dot(lo, o)
    put_parts(jnp.concatenate([total, pieces], axis=1), outs)


def combine_grads_kernel(o_ref, back_ref, *outs):
    put_parts(dot(back_ref[...], o_ref[...]), outs)


def forward_kernel(x_ref, wg_ref, wu_ref, wd_ref, slope_ref, swish_ref, hidden_ref, out_ref):
    x = x_ref[...]
    gate = dot(x, wg_ref[...])
    up = dot(x, wu_ref[...])
    squash = jax.nn.sigmoid(gate)
    swish = gate * squash
    hidden = (swish * up).astype(BF16)
    hidden_ref[...] = hidden
    hidden_ref.send()
    swish_ref[...] = swish
    swish_ref.send()
    slope_ref[...] = up * squash * (1.0 + gate * (1.0 - squash))
    slope_ref.send()
    for row in range(0, x_ref.shape[0], ROWS):
        here = slice(row, row + ROWS)
        out_ref[here] = dot(hidden[here], wd_ref[...]).astype(BF16)
        out_ref.send(here)


def backward_kernel(g_ref, wd_ref, slope_ref, swish_ref, wg_ref, wu_ref, gg_ref, ug_ref, dx_ref):
    hidden_grad = dot_nt(g_ref[...], wd_ref[...])
    gate_grad = (hidden_grad * slope_ref[...]).astype(BF16)
    gg_ref[...] = gate_grad
    gg_ref.send()
    up_grad = (hidden_grad * swish_ref[...]).astype(BF16)
    ug_ref[...] = up_grad
    ug_ref.send()
    for row in range(0, g_ref.shape[0], ROWS):
        here = slice(row, row + ROWS)
        part = dot_nt(gate_grad[here], wg_ref[...]) + dot_nt(up_grad[here], wu_ref[...])
        dx_ref[here] = part.astype(BF16)
        dx_ref.send(here)


def weight_grad_kernel(x_ref, pair_ref, hidden_ref, g_ref, *refs):
    received, (gu_ref, wd_ref) = refs[:-2], refs[-2:]
    f = hidden_ref.shape[1]
    for column in range(0, x_ref.shape[1], COLUMNS):
        here = slice(column, column + COLUMNS)
        v = dot_tn(x_ref[:, here], pair_ref[...])
        for i in range(2):
            one = v[:, i * f : (i + 1) * f]
            if received:
                one = one + received[0][i, here].astype(F32)
            gu_ref[i, here] = one.astype(BF16)
            gu_ref.send((i, here))
    v = dot_tn(hidden_ref[...], g_ref[...])
    if received:
        v = v + received[1][...].astype(F32)
    wd_ref[...] = v.astype(BF16)


def join_kernel(part_up, part_down, from_below, from_above, *refs):
    far, (up_ref, down_ref) = refs[:-2], refs[-2:]
    block = part_up.shape[0]
    up = part_up[...] + from_below[:block].astype(F32)
    down = part_down[...] + from_above[:block].astype(F32)
    half = far[0].shape[1]
    up_ref[:, :half] = (up[:, :half] + far[0][...].astype(F32)).astype(BF16)
    up_ref[:, half:] = up[:, half:].astype(BF16)
    down_ref[:, :half] = down[:, :half].astype(BF16)
    down_ref[:, half:] = (down[:, half:] + far[1][...].astype(F32)).astype(BF16)


def total_of(own, from_below, from_above, two_below, two_above):
    block = own.shape[0]
    total = own[...] + (from_below[block:].astype(F32) + from_above[block:].astype(F32))
    return total + (two_below[...].astype(F32) + two_above[...].astype(F32))


def finish_out_kernel(*refs):
    out_ref, prob_ref = refs[-2:]
    total = total_of(*refs[:-2])
    d = out_ref.shape[1]
    out_ref[...] = total[:, :d].astype(BF16)
    pieces = total[:, d:].T
    prob_ref[...] = pieces[0:TOP] + (pieces[TOP : 2 * TOP] + pieces[2 * TOP : 3 * TOP])


def finish_grads_kernel(*refs):
    refs[-1][...] = total_of(*refs[:-1]).astype(BF16)


def nothing_kernel(first, second, out):
    pass


def cost(flops, args, out_shapes):
    nbytes = sum(a.size * a.dtype.itemsize for a in [*args, *out_shapes])
    return pl.CostEstimate(flops=flops, bytes_accessed=nbytes, transcendentals=0)


class Arriving:
    def __init__(self, ref, copies):
        self.ref, self.copies, self.later = ref, copies, []
        self.shape, self.dtype = ref.shape, ref.dtype

    def start(self):
        for copy in self.copies:
            copy.start()

    def settle(self):
        for copy in self.copies:
            copy.wait()
        for buffer in self.later:
            buffer.start()
        self.copies, self.later = [], []

    def __getitem__(self, at):
        self.settle()
        return self.ref[at]


class Leaving:
    def __init__(self, ref, target, next_sem):
        self.ref, self.target, self.next_sem, self.copies = ref, target, next_sem, []
        self.shape, self.dtype = ref.shape, ref.dtype

    def __setitem__(self, at, value):
        self.ref[at] = value

    def send(self, at=None):
        source, target = (self.ref, self.target) if at is None else (self.ref.at[at], self.target.at[at])
        copy = pltpu.make_async_copy(source, target, self.next_sem())
        copy.start()
        self.copies.append(copy)


MOST_SENDS = 16


def staged(kernel, scalars, near, read, unread, loads, eager, made, *refs):
    first, rest = refs[: scalars + near], refs[scalars + near :]
    ins, rest = rest[:read], rest[read + unread :]
    outs, rest = rest[:made], rest[made:]
    held, rest = rest[: len(loads)], rest[len(loads) :]
    made_here, (in_sems, out_sems) = rest[:-2], rest[-2:]
    arriving, count = [], 0
    for here, (_, _, pieces) in zip(held, loads):
        copies = []
        for operand, source_at, target_at in pieces:
            source = ins[operand] if source_at is None else ins[operand].at[source_at]
            target = here if target_at is None else here.at[target_at]
            copies.append(pltpu.make_async_copy(source, target, in_sems.at[count]))
            count += 1
        arriving.append(Arriving(here, copies))
    for buffer in arriving[:eager]:
        buffer.start()
    if arriving[eager:]:
        arriving[eager - 1].later = arriving[eager:]
    sems = iter(range(MOST_SENDS))
    leaving = [Leaving(h, o, lambda: out_sems.at[next(sems)]) for h, o in zip(made_here, outs)]
    kernel(*first, *arriving, *(leaving or outs))
    for buffer in leaving:
        if not buffer.copies:
            buffer.send()
    for buffer in arriving:
        buffer.settle()
    for buffer in leaving:
        for copy in buffer.copies:
            copy.wait()


def call(
    kernel, out_shapes, args, scalars=0, near=0, unread=0, loads=None, eager=99, flops=0, vmem=63,
    near_out=False
):
    smem = pl.BlockSpec(memory_space=pltpu.SMEM)
    whole = pl.BlockSpec(memory_space=pltpu.VMEM)
    hbm = pl.BlockSpec(memory_space=pl.ANY)
    shapes = [jax.ShapeDtypeStruct(s, t) for s, t in out_shapes]
    read = len(args) - scalars - near - unread
    ins = args[scalars + near : scalars + near + read]
    if loads is None:
        loads = [(a.shape, a.dtype, [(i, None, None)]) for i, a in enumerate(ins)]
    copies = sum(len(pieces) for _, _, pieces in loads)
    counted = args[scalars : len(args) - unread] if flops else []
    return pl.pallas_call(
        functools.partial(
            staged, kernel, scalars, near, read, unread, loads, eager, len(shapes)
        ),
        out_shape=shapes,
        in_specs=[smem] * scalars + [whole] * near + [hbm] * (read + unread),
        out_specs=[whole if near_out else hbm] * len(shapes),
        scratch_shapes=[pltpu.VMEM(shape, dtype) for shape, dtype, _ in loads]
        + [pltpu.VMEM(a.shape, a.dtype) for a in shapes if not near_out]
        + [pltpu.SemaphoreType.DMA((copies,)), pltpu.SemaphoreType.DMA((MOST_SENDS,))],
        compiler_params=pltpu.CompilerParams(vmem_limit_bytes=vmem * MIB),
        cost_estimate=cost(flops, counted, shapes if flops else []),
    )(*args)


def dropping(kernel, read, unread, *refs):
    kernel(*refs[:read], *refs[read + unread :])


def small(kernel, out_shapes, args, unread=0, vmem=8, flops=0):
    whole = pl.BlockSpec(memory_space=pltpu.VMEM)
    hbm = pl.BlockSpec(memory_space=pl.ANY)
    shapes = [jax.ShapeDtypeStruct(s, t) for s, t in out_shapes]
    read = len(args) - unread
    return pl.pallas_call(
        functools.partial(dropping, kernel, read, unread),
        out_shape=shapes,
        in_specs=[whole] * read + [hbm] * unread,
        out_specs=[whole] * len(shapes),
        compiler_params=pltpu.CompilerParams(vmem_limit_bytes=vmem * MIB),
        cost_estimate=cost(flops, args[:read], shapes),
    )(*args)


def beside(shape, one, other, at=None):
    width = shape[1]
    return (
        (shape[0], 2 * width),
        BF16,
        [
            (one, at, (slice(None), slice(0, width))),
            (other, at, (slice(None), slice(width, 2 * width))),
        ],
    )


def below(shape, one, other):
    height = shape[0]
    return (
        (2 * height, shape[1]),
        BF16,
        [(one, None, slice(0, height)), (other, None, slice(height, 2 * height))],
    )


def forward(x, gu, wd):
    rows, d = x.shape
    f = wd[0].shape[0]
    wide = (rows, 2 * f)
    return call(
        forward_kernel,
        [(wide, F32), (wide, F32), (wide, BF16), ((rows, d), BF16)],
        [x, *gu, *wd],
        loads=[
            (x.shape, BF16, [(0, None, None)]),
            beside((d, f), 1, 2, 0),
            beside((d, f), 1, 2, 1),
            below((f, d), 3, 4),
        ],
        flops=12 * rows * d * f,
    )


def backward(g, slope, swish, gu, wd):
    rows, d = g.shape
    f = wd[0].shape[0]
    return call(
        backward_kernel,
        [((rows, 2 * f), BF16), ((rows, 2 * f), BF16), ((rows, d), BF16)],
        [g, slope, swish, *gu, *wd],
        loads=[
            (g.shape, BF16, [(0, None, None)]),
            below((f, d), 5, 6),
            (slope.shape, F32, [(1, None, None)]),
            (swish.shape, F32, [(2, None, None)]),
            beside((d, f), 3, 4, 0),
            beside((d, f), 3, 4, 1),
        ],
        flops=12 * rows * d * f,
    )


def weight_grads(x, g, gg, ug, hidden, half, received=()):
    rows, d = x.shape
    f = gg.shape[1] // 2
    mine = (slice(None), slice(half * f, (half + 1) * f))
    pair = [(2, mine, (slice(None), slice(0, f))), (3, mine, (slice(None), slice(f, 2 * f)))]
    return call(
        weight_grad_kernel,
        [((2, d, f), BF16), ((f, d), BF16)],
        [x, g, gg, ug, hidden, *received],
        loads=[
            (x.shape, BF16, [(0, None, None)]),
            ((rows, 2 * f), BF16, pair),
            ((rows, f), BF16, [(4, mine, None)]),
            (g.shape, BF16, [(1, None, None)]),
        ]
        + [(v.shape, BF16, [(5 + i, None, None)]) for i, v in enumerate(received)],
        flops=0 if received else 6 * rows * d * f,
    )


def after(value, earlier):
    hbm = pl.BlockSpec(memory_space=pl.ANY)
    return pl.pallas_call(
        nothing_kernel,
        out_shape=jax.ShapeDtypeStruct(value.shape, value.dtype),
        in_specs=[hbm, hbm],
        out_specs=hbm,
        input_output_aliases={0: 0},
        cost_estimate=pl.CostEstimate(flops=0, bytes_accessed=0, transcendentals=0),
    )(value, earlier)


def shift_z(v, step):
    return lax.ppermute(v, "z", [(i, (i + step) % NZ) for i in range(NZ)])


def gather_z(own):
    held = {0: own}
    for hop in range(1, 5):
        if hop < 4:
            held[-hop] = shift_z(held[1 - hop], 1)
        held[hop] = shift_z(held[hop - 1], -1)
    return [held[r] for r in ORDER]


def part_shapes(t, width):
    half = (width // 2 + 127) // 128 * 128
    return (
        [((t, width), F32)] * 3
        + [((2 * t, width), BF16)] * 2
        + [((t, half), BF16), ((t, width - half), BF16)]
    )


def scatter_z(parts, finish, out_shapes, run, earlier=()):
    own, two_up, two_down, up, down, *far = parts
    from_below, from_above = shift_z(up, 1), shift_z(down, -1)
    far = [shift_z(v, step) for v, step in zip(far, (2, -2))]
    two_up, two_down = run(
        join_kernel,
        [(two_up.shape, BF16)] * 2,
        [two_up, two_down, from_below, from_above, *far, *earlier],
        unread=len(earlier),
    )
    two_below, two_above = shift_z(two_up, 2), shift_z(two_down, -2)
    return two_up, run(finish, out_shapes, [own, from_below, from_above, two_below, two_above])


def swap_dp(v):
    return lax.ppermute(v, "dp", [(0, 1), (1, 0)])


def exchange_plane(rows):
    r, d = rows.shape
    out = lax.all_to_all(
        rows.reshape(PLANE, r // PLANE, d), ("x", "y"), split_axis=0, concat_axis=0, tiled=True
    )
    return out.reshape(r, d)


def on_device(tokens, expert_ids, route_weight, w_gate_up, w_down, out_grad):
    t, d = tokens.shape[1:]
    n = t * NZ
    rows = PLANE * NZ * SLOTS
    z = lax.axis_index("z").astype(jnp.int32).reshape(1)

    gu = (w_gate_up[0], swap_dp(w_gate_up[0]))
    wd = (w_down[0], swap_dp(w_down[0]))
    (blob,) = call(
        blob_kernel, [((t, d + 128), BF16)], [expert_ids[0].T, route_weight[0].T, tokens[0]]
    )
    blobs = gather_z(blob)
    send_x, placing, row_weight, ids = call(
        place_tokens_kernel,
        [((rows, d), BF16), ((rows, n), BF16), ((rows, 128), F32), ((TOP, n), F32)],
        [z, *blobs, gu[1], wd[1]],
        scalars=1,
        near=NZ,
        unread=2,
        vmem=62,
        flops=2 * rows * n * d,
    )
    x = exchange_plane(send_x)
    grads = gather_z(out_grad[0])
    (send_g,) = call(
        place_grads_kernel,
        [((rows, d), BF16)],
        [*grads, placing, row_weight],
        near=NZ,
        flops=2 * rows * n * d,
        vmem=62,
    )
    g = exchange_plane(send_g)
    slope, swish, hidden, out_rows = forward(x, gu, wd)
    o = exchange_plane(after(out_rows, g))
    gate_grad, up_grad, grad_rows = backward(g, slope, swish, gu, wd)
    grad_rows = after(grad_rows, o)
    dx = exchange_plane(grad_rows)

    away = weight_grads(x, g, gate_grad, up_grad, hidden, 1)
    received = [swap_dp(v) for v in away]
    grad_gate_up, grad_down = weight_grads(x, g, gate_grad, up_grad, hidden, 0, received)

    back, *parts = call(
        combine_out_kernel,
        [((n, rows), BF16)] + part_shapes(t, d + 128),
        [z, placing, row_weight, ids, o, send_g, away[0], grad_rows],
        scalars=1,
        unread=2,
    )
    midway, (layer_out, prob_grad) = scatter_z(
        parts, finish_out_kernel, [((t, d), BF16), ((TOP, t), F32)], call, [grad_gate_up]
    )
    parts = call(
        combine_grads_kernel,
        part_shapes(t, d),
        [after(dx, midway), back],
        near_out=True,
        vmem=61,
        flops=2 * rows * n * d,
    )
    _, (token_grad,) = scatter_z(parts, finish_grads_kernel, [((t, d), BF16)], small)
    return (
        layer_out[None],
        token_grad[None],
        prob_grad.T[None],
        grad_gate_up[None],
        grad_down[None],
    )


def solution(mesh):
    fine = Mesh(mesh.devices.reshape(NX, NY, NZ, 2), ("x", "y", "z", "dp"))
    expert = ("x", "y", "z")
    by_token = P("dp", expert, None)
    specs = (by_token, by_token, by_token, P(expert, None, None, "dp"), P(expert, "dp", None))
    return jax.shard_map(
        on_device,
        mesh=fine,
        in_specs=specs + (by_token,),
        out_specs=(by_token, by_token, by_token, specs[3], specs[4]),
        check_vma=False,
    )
```

```python
import functools

import jax
import jax.numpy as jnp
import numpy as np
from jax import lax
from jax.experimental import pallas as pl
from jax.experimental.pallas import tpu as pltpu
from jax.sharding import Mesh, PartitionSpec as P

F32 = jnp.float32
BF16 = jnp.bfloat16
NX, NY, NZ = 4, 4, 8
PLANE = NX * NY
SLOTS = 4
TOP = 8
MIB = 1 << 20
ROWS = 256
COLUMNS = 1024


def dot(a, b):
    return jnp.dot(a, b, preferred_element_type=F32)


def dot_nt(a, b):
    return lax.dot_general(a, b, (((1,), (1,)), ((), ())), preferred_element_type=F32)


def dot_tn(a, b):
    return lax.dot_general(a, b, (((0,), (0,)), ((), ())), preferred_element_type=F32)


def split3(v):
    hi = v.astype(BF16)
    rest = v - hi.astype(F32)
    mid = rest.astype(BF16)
    lo = (rest - mid.astype(F32)).astype(BF16)
    return hi, mid, lo


ORDER = (0, -1, 1, -2, 2, -3, 3, 4)


def place(meta, z):
    n = meta.shape[0]
    rows = PLANE * NZ * SLOTS
    turned = meta.T
    ids = turned[0:TOP]
    weights = turned[TOP : 2 * TOP] + turned[2 * TOP : 3 * TOP] + turned[3 * TOP : 4 * TOP]
    expert = (lax.broadcasted_iota(jnp.int32, (PLANE, n), 0) * NZ + z).astype(F32)
    named = jnp.zeros((PLANE, n), F32)
    weight = jnp.zeros((PLANE, n), F32)
    for k in range(TOP):
        hit = ids[k : k + 1] == expert
        named = jnp.where(hit, 1.0, named)
        weight = jnp.where(hit, weights[k : k + 1], weight)
    block = n // NZ
    shift = block.bit_length() - 1
    from_t = lax.broadcasted_iota(jnp.int32, (n, n), 0)
    to_t = lax.broadcasted_iota(jnp.int32, (n, n), 1)
    same = lax.shift_right_logical(from_t, shift) == lax.shift_right_logical(to_t, shift)
    before = jnp.where(same & (from_t < to_t), 1.0, 0.0).astype(BF16)
    rank = dot(named.astype(BF16), before)
    rank = jnp.where(named > 0.5, rank, -1.0)

    def spread(v):
        return jnp.broadcast_to(v[:, None, :], (PLANE, NZ * SLOTS, n)).reshape(rows, n)

    row = lax.broadcasted_iota(jnp.int32, (rows, n), 0)
    col = lax.broadcasted_iota(jnp.int32, (rows, n), 1)
    row_block = lax.shift_right_logical(row, 2) & (NZ - 1)
    slot = (row & (SLOTS - 1)).astype(F32)
    here = (spread(rank) == slot) & (lax.shift_right_logical(col, shift) == row_block)
    placing = jnp.where(here, 1.0, 0.0)
    row_weight = jnp.sum(jnp.where(here, spread(weight), 0.0), axis=1, keepdims=True)
    return placing, row_weight, ids


def blob_kernel(ids_ref, weight_ref, tokens_ref, blob_ref):
    t, d = tokens_ref.shape
    pieces = [v.astype(F32) for v in split3(weight_ref[...])]
    rest = jnp.zeros((128 - 4 * TOP, t), F32)
    meta = jnp.concatenate([ids_ref[...].astype(F32), *pieces, rest], axis=0)
    blob_ref[:, :d] = tokens_ref[...]
    blob_ref[:, d:] = meta.T.astype(BF16)


def place_tokens_kernel(z_ref, *refs):
    blobs, (x_ref, placing_ref, weight_ref, ids_ref) = refs[:NZ], refs[NZ:]
    d = x_ref.shape[1]
    meta = jnp.concatenate([b[:, d:].astype(F32) for b in blobs], axis=0)
    placing, row_weight, ids = place(meta, z_ref[0])
    placing = placing.astype(BF16)
    placing_ref[...] = placing
    weight_ref[...] = jnp.broadcast_to(row_weight, weight_ref.shape)
    ids_ref[...] = ids
    tokens = jnp.concatenate([b[:, :d] for b in blobs], axis=0)
    for row in range(0, x_ref.shape[0], ROWS):
        here = slice(row, row + ROWS)
        x_ref[here] = dot(placing[here], tokens).astype(BF16)
        x_ref.send(here)


def place_grads_kernel(*refs):
    grads, (placing_ref, weight_ref, g_ref) = refs[:NZ], refs[NZ:]
    placing = placing_ref[...]
    og = jnp.concatenate([b[...] for b in grads], axis=0)
    for row in range(0, g_ref.shape[0], ROWS):
        here = slice(row, row + ROWS)
        g_ref[here] = (dot(placing[here], og) * weight_ref[here, 0:1]).astype(BF16)
        g_ref.send(here)


def put_parts(total, outs):
    block = total.shape[0] // NZ
    part = {r: total[i * block : (i + 1) * block] for i, r in enumerate(ORDER)}
    own, two_up, two_down, up, down, *far = outs
    half = far[0].shape[1]
    own[...] = part[0]
    two_up[...] = part[2]
    two_down[...] = part[-2]
    for out, sign in ((up, 1), (down, -1)):
        out[:block] = part[3 * sign].astype(BF16)
        out[block:] = part[sign].astype(BF16)
    last = part[4].astype(BF16)
    far[0][...] = last[:, :half]
    far[1][...] = last[:, half:]


def combine_out_kernel(
    z_ref, placing_ref, weight_ref, ids_ref, o_ref, g_ref, back_ref, *outs
):
    rows = o_ref.shape[0]
    placing = placing_ref[...].astype(F32)
    n = placing.shape[1]
    row_weight = weight_ref[:, 0:1]
    back_ref[...] = placing.T.astype(BF16)
    back_ref.send()
    weighted = (placing * row_weight).T
    hi = weighted.astype(BF16)
    lo = (weighted - hi.astype(F32)).astype(BF16)
    o = o_ref[...]
    inverse = jnp.where(row_weight > 0.0, 1.0 / jnp.where(row_weight > 0.0, row_weight, 1.0), 0.0)
    dots = jnp.sum(g_ref[...].astype(F32) * o.astype(F32), axis=1, keepdims=True) * inverse
    per_expert = jnp.sum(
        (placing * dots).reshape(PLANE, rows // PLANE, n), axis=1
    )
    expert = (lax.broadcasted_iota(jnp.int32, (PLANE, n), 0) * NZ + z_ref[0]).astype(F32)
    ids = ids_ref[...]
    probs = jnp.concatenate(
        [
            jnp.sum(jnp.where(ids[k : k + 1] == expert, per_expert, 0.0), axis=0, keepdims=True)
            for k in range(TOP)
        ],
        axis=0,
    )
    pieces = [v.astype(F32) for v in split3(probs)]
    pieces = jnp.concatenate([*pieces, jnp.zeros((128 - 3 * TOP, n), F32)], axis=0).T
    total = dot(hi, o) + dot(lo, o)
    put_parts(jnp.concatenate([total, pieces], axis=1), outs)


def combine_grads_kernel(o_ref, back_ref, *outs):
    put_parts(dot(back_ref[...], o_ref[...]), outs)


def forward_kernel(x_ref, wg_ref, wu_ref, wd_ref, slope_ref, swish_ref, hidden_ref, out_ref):
    x = x_ref[...]
    gate = dot(x, wg_ref[...])
    up = dot(x, wu_ref[...])
    squash = jax.nn.sigmoid(gate)
    swish = gate * squash
    hidden = (swish * up).astype(BF16)
    hidden_ref[...] = hidden
    hidden_ref.send()
    swish_ref[...] = swish
    swish_ref.send()
    slope_ref[...] = up * squash * (1.0 + gate * (1.0 - squash))
    slope_ref.send()
    for row in range(0, x_ref.shape[0], ROWS):
        here = slice(row, row + ROWS)
        out_ref[here] = dot(hidden[here], wd_ref[...]).astype(BF16)
        out_ref.send(here)


def backward_kernel(g_ref, wd_ref, slope_ref, swish_ref, wg_ref, wu_ref, gg_ref, ug_ref, dx_ref):
    hidden_grad = dot_nt(g_ref[...], wd_ref[...])
    gate_grad = (hidden_grad * slope_ref[...]).astype(BF16)
    gg_ref[...] = gate_grad
    gg_ref.send()
    up_grad = (hidden_grad * swish_ref[...]).astype(BF16)
    ug_ref[...] = up_grad
    ug_ref.send()
    for row in range(0, g_ref.shape[0], ROWS):
        here = slice(row, row + ROWS)
        part = dot_nt(gate_grad[here], wg_ref[...]) + dot_nt(up_grad[here], wu_ref[...])
        dx_ref[here] = part.astype(BF16)
        dx_ref.send(here)


def weight_grad_kernel(x_ref, pair_ref, hidden_ref, g_ref, *refs):
    received, (gu_ref, wd_ref) = refs[:-2], refs[-2:]
    f = hidden_ref.shape[1]
    for column in range(0, x_ref.shape[1], COLUMNS):
        here = slice(column, column + COLUMNS)
        v = dot_tn(x_ref[:, here], pair_ref[...])
        for i in range(2):
            one = v[:, i * f : (i + 1) * f]
            if received:
                one = one + received[0][i, here].astype(F32)
            gu_ref[i, here] = one.astype(BF16)
            gu_ref.send((i, here))
    v = dot_tn(hidden_ref[...], g_ref[...])
    if received:
        v = v + received[1][...].astype(F32)
    wd_ref[...] = v.astype(BF16)


def join_kernel(part_up, part_down, from_below, from_above, *refs):
    far, (up_ref, down_ref) = refs[:-2], refs[-2:]
    block = part_up.shape[0]
    up = part_up[...] + from_below[:block].astype(F32)
    down = part_down[...] + from_above[:block].astype(F32)
    half = far[0].shape[1]
    up_ref[:, :half] = (up[:, :half] + far[0][...].astype(F32)).astype(BF16)
    up_ref[:, half:] = up[:, half:].astype(BF16)
    down_ref[:, :half] = down[:, :half].astype(BF16)
    down_ref[:, half:] = (down[:, half:] + far[1][...].astype(F32)).astype(BF16)


def total_of(own, from_below, from_above, two_below, two_above):
    block = own.shape[0]
    total = own[...] + (from_below[block:].astype(F32) + from_above[block:].astype(F32))
    return total + (two_below[...].astype(F32) + two_above[...].astype(F32))


def finish_out_kernel(*refs):
    out_ref, prob_ref = refs[-2:]
    total = total_of(*refs[:-2])
    d = out_ref.shape[1]
    out_ref[...] = total[:, :d].astype(BF16)
    pieces = total[:, d:].T
    prob_ref[...] = pieces[0:TOP] + (pieces[TOP : 2 * TOP] + pieces[2 * TOP : 3 * TOP])


def finish_grads_kernel(*refs):
    refs[-1][...] = total_of(*refs[:-1]).astype(BF16)


def nothing_kernel(first, second, out):
    pass


def cost(flops, args, out_shapes):
    nbytes = sum(a.size * a.dtype.itemsize for a in [*args, *out_shapes])
    return pl.CostEstimate(flops=flops, bytes_accessed=nbytes, transcendentals=0)


class Arriving:
    def __init__(self, ref, copies):
        self.ref, self.copies, self.later = ref, copies, []
        self.shape, self.dtype = ref.shape, ref.dtype

    def start(self):
        for copy in self.copies:
            copy.start()

    def settle(self):
        for copy in self.copies:
            copy.wait()
        for buffer in self.later:
            buffer.start()
        self.copies, self.later = [], []

    def __getitem__(self, at):
        self.settle()
        return self.ref[at]


class Leaving:
    def __init__(self, ref, target, next_sem):
        self.ref, self.target, self.next_sem, self.copies = ref, target, next_sem, []
        self.shape, self.dtype = ref.shape, ref.dtype

    def __setitem__(self, at, value):
        self.ref[at] = value

    def send(self, at=None):
        source, target = (self.ref, self.target) if at is None else (self.ref.at[at], self.target.at[at])
        copy = pltpu.make_async_copy(source, target, self.next_sem())
        copy.start()
        self.copies.append(copy)


MOST_SENDS = 16


def staged(kernel, scalars, near, read, unread, loads, eager, made, *refs):
    first, rest = refs[: scalars + near], refs[scalars + near :]
    ins, rest = rest[:read], rest[read + unread :]
    outs, rest = rest[:made], rest[made:]
    held, rest = rest[: len(loads)], rest[len(loads) :]
    made_here, (in_sems, out_sems) = rest[:-2], rest[-2:]
    arriving, count = [], 0
    for here, (_, _, pieces) in zip(held, loads):
        copies = []
        for operand, source_at, target_at in pieces:
            source = ins[operand] if source_at is None else ins[operand].at[source_at]
            target = here if target_at is None else here.at[target_at]
            copies.append(pltpu.make_async_copy(source, target, in_sems.at[count]))
            count += 1
        arriving.append(Arriving(here, copies))
    for buffer in arriving[:eager]:
        buffer.start()
    if arriving[eager:]:
        arriving[eager - 1].later = arriving[eager:]
    sems = iter(range(MOST_SENDS))
    leaving = [Leaving(h, o, lambda: out_sems.at[next(sems)]) for h, o in zip(made_here, outs)]
    kernel(*first, *arriving, *(leaving or outs))
    for buffer in leaving:
        if not buffer.copies:
            buffer.send()
    for buffer in arriving:
        buffer.settle()
    for buffer in leaving:
        for copy in buffer.copies:
            copy.wait()


def call(
    kernel, out_shapes, args, scalars=0, near=0, unread=0, loads=None, eager=99, flops=0, vmem=63,
    near_out=False
):
    smem = pl.BlockSpec(memory_space=pltpu.SMEM)
    whole = pl.BlockSpec(memory_space=pltpu.VMEM)
    hbm = pl.BlockSpec(memory_space=pl.ANY)
    shapes = [jax.ShapeDtypeStruct(s, t) for s, t in out_shapes]
    read = len(args) - scalars - near - unread
    ins = args[scalars + near : scalars + near + read]
    if loads is None:
        loads = [(a.shape, a.dtype, [(i, None, None)]) for i, a in enumerate(ins)]
    copies = sum(len(pieces) for _, _, pieces in loads)
    counted = args[scalars : len(args) - unread] if flops else []
    return pl.pallas_call(
        functools.partial(
            staged, kernel, scalars, near, read, unread, loads, eager, len(shapes)
        ),
        out_shape=shapes,
        in_specs=[smem] * scalars + [whole] * near + [hbm] * (read + unread),
        out_specs=[whole if near_out else hbm] * len(shapes),
        scratch_shapes=[pltpu.VMEM(shape, dtype) for shape, dtype, _ in loads]
        + [pltpu.VMEM(a.shape, a.dtype) for a in shapes if not near_out]
        + [pltpu.SemaphoreType.DMA((copies,)), pltpu.SemaphoreType.DMA((MOST_SENDS,))],
        compiler_params=pltpu.CompilerParams(vmem_limit_bytes=vmem * MIB),
        cost_estimate=cost(flops, counted, shapes if flops else []),
    )(*args)


def dropping(kernel, read, unread, *refs):
    kernel(*refs[:read], *refs[read + unread :])


def small(kernel, out_shapes, args, unread=0, vmem=8, flops=0):
    whole = pl.BlockSpec(memory_space=pltpu.VMEM)
    hbm = pl.BlockSpec(memory_space=pl.ANY)
    shapes = [jax.ShapeDtypeStruct(s, t) for s, t in out_shapes]
    read = len(args) - unread
    return pl.pallas_call(
        functools.partial(dropping, kernel, read, unread),
        out_shape=shapes,
        in_specs=[whole] * read + [hbm] * unread,
        out_specs=[whole] * len(shapes),
        compiler_params=pltpu.CompilerParams(vmem_limit_bytes=vmem * MIB),
        cost_estimate=cost(flops, args[:read], shapes),
    )(*args)


def beside(shape, one, other, at=None):
    width = shape[1]
    return (
        (shape[0], 2 * width),
        BF16,
        [
            (one, at, (slice(None), slice(0, width))),
            (other, at, (slice(None), slice(width, 2 * width))),
        ],
    )


def below(shape, one, other):
    height = shape[0]
    return (
        (2 * height, shape[1]),
        BF16,
        [(one, None, slice(0, height)), (other, None, slice(height, 2 * height))],
    )


def forward(x, gu, wd):
    rows, d = x.shape
    f = wd[0].shape[0]
    wide = (rows, 2 * f)
    return call(
        forward_kernel,
        [(wide, F32), (wide, F32), (wide, BF16), ((rows, d), BF16)],
        [x, *gu, *wd],
        loads=[
            (x.shape, BF16, [(0, None, None)]),
            beside((d, f), 1, 2, 0),
            beside((d, f), 1, 2, 1),
            below((f, d), 3, 4),
        ],
        flops=12 * rows * d * f,
    )


def backward(g, slope, swish, gu, wd):
    rows, d = g.shape
    f = wd[0].shape[0]
    return call(
        backward_kernel,
        [((rows, 2 * f), BF16), ((rows, 2 * f), BF16), ((rows, d), BF16)],
        [g, slope, swish, *gu, *wd],
        loads=[
            (g.shape, BF16, [(0, None, None)]),
            below((f, d), 5, 6),
            (slope.shape, F32, [(1, None, None)]),
            (swish.shape, F32, [(2, None, None)]),
            beside((d, f), 3, 4, 0),
            beside((d, f), 3, 4, 1),
        ],
        flops=12 * rows * d * f,
    )


def weight_grads(x, g, gg, ug, hidden, half, received=()):
    rows, d = x.shape
    f = gg.shape[1] // 2
    mine = (slice(None), slice(half * f, (half + 1) * f))
    pair = [(2, mine, (slice(None), slice(0, f))), (3, mine, (slice(None), slice(f, 2 * f)))]
    return call(
        weight_grad_kernel,
        [((2, d, f), BF16), ((f, d), BF16)],
        [x, g, gg, ug, hidden, *received],
        loads=[
            (x.shape, BF16, [(0, None, None)]),
            ((rows, 2 * f), BF16, pair),
            ((rows, f), BF16, [(4, mine, None)]),
            (g.shape, BF16, [(1, None, None)]),
        ]
        + [(v.shape, BF16, [(5 + i, None, None)]) for i, v in enumerate(received)],
        flops=0 if received else 6 * rows * d * f,
    )


def after(value, earlier):
    hbm = pl.BlockSpec(memory_space=pl.ANY)
    return pl.pallas_call(
        nothing_kernel,
        out_shape=jax.ShapeDtypeStruct(value.shape, value.dtype),
        in_specs=[hbm, hbm],
        out_specs=hbm,
        input_output_aliases={0: 0},
        cost_estimate=pl.CostEstimate(flops=0, bytes_accessed=0, transcendentals=0),
    )(value, earlier)


def shift_z(v, step):
    return lax.ppermute(v, "z", [(i, (i + step) % NZ) for i in range(NZ)])


def gather_z(own):
    held = {0: own}
    for hop in range(1, 5):
        if hop < 4:
            held[-hop] = shift_z(held[1 - hop], 1)
        held[hop] = shift_z(held[hop - 1], -1)
    return [held[r] for r in ORDER]


def part_shapes(t, width):
    half = (width // 2 + 127) // 128 * 128
    return (
        [((t, width), F32)] * 3
        + [((2 * t, width), BF16)] * 2
        + [((t, half), BF16), ((t, width - half), BF16)]
    )


def scatter_z(parts, finish, out_shapes, run, earlier=()):
    own, two_up, two_down, up, down, *far = parts
    from_below, from_above = shift_z(up, 1), shift_z(down, -1)
    far = [shift_z(v, step) for v, step in zip(far, (2, -2))]
    two_up, two_down = run(
        join_kernel,
        [(two_up.shape, BF16)] * 2,
        [two_up, two_down, from_below, from_above, *far, *earlier],
        unread=len(earlier),
    )
    two_below, two_above = shift_z(two_up, 2), shift_z(two_down, -2)
    return two_up, small(finish, out_shapes, [own, from_below, from_above, two_below, two_above])


def swap_dp(v):
    return lax.ppermute(v, "dp", [(0, 1), (1, 0)])


def exchange_plane(rows):
    r, d = rows.shape
    out = lax.all_to_all(
        rows.reshape(PLANE, r // PLANE, d), ("x", "y"), split_axis=0, concat_axis=0, tiled=True
    )
    return out.reshape(r, d)


def on_device(tokens, expert_ids, route_weight, w_gate_up, w_down, out_grad):
    t, d = tokens.shape[1:]
    n = t * NZ
    rows = PLANE * NZ * SLOTS
    z = lax.axis_index("z").astype(jnp.int32).reshape(1)

    gu = (w_gate_up[0], swap_dp(w_gate_up[0]))
    wd = (w_down[0], swap_dp(w_down[0]))
    (blob,) = call(
        blob_kernel, [((t, d + 128), BF16)], [expert_ids[0].T, route_weight[0].T, tokens[0]]
    )
    blobs = gather_z(blob)
    send_x, placing, row_weight, ids = call(
        place_tokens_kernel,
        [((rows, d), BF16), ((rows, n), BF16), ((rows, 128), F32), ((TOP, n), F32)],
        [z, *blobs, gu[1], wd[1]],
        scalars=1,
        near=NZ,
        unread=2,
        vmem=62,
        flops=2 * rows * n * d,
    )
    x = exchange_plane(send_x)
    grads = gather_z(out_grad[0])
    (send_g,) = call(
        place_grads_kernel,
        [((rows, d), BF16)],
        [*grads, placing, row_weight],
        near=NZ + 2,
        flops=2 * rows * n * d,
        vmem=62,
    )
    g = exchange_plane(send_g)
    slope, swish, hidden, out_rows = forward(x, gu, wd)
    o = exchange_plane(after(out_rows, g))
    gate_grad, up_grad, grad_rows = backward(g, slope, swish, gu, wd)
    grad_rows = after(grad_rows, o)
    dx = exchange_plane(grad_rows)

    away = weight_grads(x, g, gate_grad, up_grad, hidden, 1)
    received = [swap_dp(v) for v in away]
    grad_gate_up, grad_down = weight_grads(x, g, gate_grad, up_grad, hidden, 0, received)

    back, *parts = call(
        combine_out_kernel,
        [((n, rows), BF16)] + part_shapes(t, d + 128),
        [z, placing, row_weight, ids, o, send_g, away[0], grad_rows],
        scalars=1,
        unread=2,
    )
    midway, (layer_out, prob_grad) = scatter_z(
        parts, finish_out_kernel, [((t, d), BF16), ((TOP, t), F32)], call, [grad_gate_up]
    )
    parts = call(
        combine_grads_kernel,
        part_shapes(t, d),
        [after(dx, midway), back],
        near_out=True,
        vmem=48,
        flops=2 * rows * n * d,
    )
    _, (token_grad,) = scatter_z(parts, finish_grads_kernel, [((t, d), BF16)], small)
    return (
        layer_out[None],
        token_grad[None],
        prob_grad.T[None],
        grad_gate_up[None],
        grad_down[None],
    )


def solution(mesh):
    fine = Mesh(mesh.devices.reshape(NX, NY, NZ, 2), ("x", "y", "z", "dp"))
    expert = ("x", "y", "z")
    by_token = P("dp", expert, None)
    specs = (by_token, by_token, by_token, P(expert, None, None, "dp"), P(expert, "dp", None))
    return jax.shard_map(
        on_device,
        mesh=fine,
        in_specs=specs + (by_token,),
        out_specs=(by_token, by_token, by_token, specs[3], specs[4]),
        check_vma=False,
    )
```

```python
import functools

import jax
import jax.numpy as jnp
import numpy as np
from jax import lax
from jax.experimental import pallas as pl
from jax.experimental.pallas import tpu as pltpu
from jax.sharding import Mesh, PartitionSpec as P

F32 = jnp.float32
BF16 = jnp.bfloat16
NX, NY, NZ = 4, 4, 8
PLANE = NX * NY
SLOTS = 4
TOP = 8
MIB = 1 << 20
ROWS = 256
COLUMNS = 1024


def dot(a, b):
    return jnp.dot(a, b, preferred_element_type=F32)


def dot_nt(a, b):
    return lax.dot_general(a, b, (((1,), (1,)), ((), ())), preferred_element_type=F32)


def dot_tn(a, b):
    return lax.dot_general(a, b, (((0,), (0,)), ((), ())), preferred_element_type=F32)


def split3(v):
    hi = v.astype(BF16)
    rest = v - hi.astype(F32)
    mid = rest.astype(BF16)
    lo = (rest - mid.astype(F32)).astype(BF16)
    return hi, mid, lo


ORDER = (0, -1, 1, -2, 2, -3, 3, 4)


def place(meta, z):
    n = meta.shape[0]
    rows = PLANE * NZ * SLOTS
    turned = meta.T
    ids = turned[0:TOP]
    weights = turned[TOP : 2 * TOP] + turned[2 * TOP : 3 * TOP] + turned[3 * TOP : 4 * TOP]
    expert = (lax.broadcasted_iota(jnp.int32, (PLANE, n), 0) * NZ + z).astype(F32)
    named = jnp.zeros((PLANE, n), F32)
    weight = jnp.zeros((PLANE, n), F32)
    for k in range(TOP):
        hit = ids[k : k + 1] == expert
        named = jnp.where(hit, 1.0, named)
        weight = jnp.where(hit, weights[k : k + 1], weight)
    block = n // NZ
    shift = block.bit_length() - 1
    from_t = lax.broadcasted_iota(jnp.int32, (n, n), 0)
    to_t = lax.broadcasted_iota(jnp.int32, (n, n), 1)
    same = lax.shift_right_logical(from_t, shift) == lax.shift_right_logical(to_t, shift)
    before = jnp.where(same & (from_t < to_t), 1.0, 0.0).astype(BF16)
    rank = dot(named.astype(BF16), before)
    rank = jnp.where(named > 0.5, rank, -1.0)

    def spread(v):
        return jnp.broadcast_to(v[:, None, :], (PLANE, NZ * SLOTS, n)).reshape(rows, n)

    row = lax.broadcasted_iota(jnp.int32, (rows, n), 0)
    col = lax.broadcasted_iota(jnp.int32, (rows, n), 1)
    row_block = lax.shift_right_logical(row, 2) & (NZ - 1)
    slot = (row & (SLOTS - 1)).astype(F32)
    here = (spread(rank) == slot) & (lax.shift_right_logical(col, shift) == row_block)
    placing = jnp.where(here, 1.0, 0.0)
    row_weight = jnp.sum(jnp.where(here, spread(weight), 0.0), axis=1, keepdims=True)
    return placing, row_weight, ids


def blob_kernel(ids_ref, weight_ref, tokens_ref, blob_ref):
    t, d = tokens_ref.shape
    pieces = [v.astype(F32) for v in split3(weight_ref[...])]
    rest = jnp.zeros((128 - 4 * TOP, t), F32)
    meta = jnp.concatenate([ids_ref[...].astype(F32), *pieces, rest], axis=0)
    blob_ref[:, :d] = tokens_ref[...]
    blob_ref[:, d:] = meta.T.astype(BF16)


def place_tokens_kernel(z_ref, *refs):
    blobs, (x_ref, placing_ref, weight_ref, ids_ref) = refs[:NZ], refs[NZ:]
    d = x_ref.shape[1]
    meta = jnp.concatenate([b[:, d:].astype(F32) for b in blobs], axis=0)
    placing, row_weight, ids = place(meta, z_ref[0])
    placing = placing.astype(BF16)
    placing_ref[...] = placing
    weight_ref[...] = jnp.broadcast_to(row_weight, weight_ref.shape)
    ids_ref[...] = ids
    for ref in (placing_ref, weight_ref, ids_ref):
        ref.send()
    tokens = jnp.concatenate([b[:, :d] for b in blobs], axis=0)
    for row in range(0, x_ref.shape[0], ROWS):
        here = slice(row, row + ROWS)
        x_ref[here] = dot(placing[here], tokens).astype(BF16)
        x_ref.send(here)


def place_grads_kernel(*refs):
    grads, (placing_ref, weight_ref, g_ref) = refs[:NZ], refs[NZ:]
    placing = placing_ref[...]
    og = jnp.concatenate([b[...] for b in grads], axis=0)
    for row in range(0, g_ref.shape[0], ROWS):
        here = slice(row, row + ROWS)
        g_ref[here] = (dot(placing[here], og) * weight_ref[here, 0:1]).astype(BF16)
        g_ref.send(here)


def put_parts(total, outs):
    block = total.shape[0] // NZ
    part = {r: total[i * block : (i + 1) * block] for i, r in enumerate(ORDER)}
    own, two_up, two_down, up, down, *far = outs
    half = far[0].shape[1]
    own[...] = part[0]
    two_up[...] = part[2]
    two_down[...] = part[-2]
    for out, sign in ((up, 1), (down, -1)):
        out[:block] = part[3 * sign].astype(BF16)
        out[block:] = part[sign].astype(BF16)
    last = part[4].astype(BF16)
    far[0][...] = last[:, :half]
    far[1][...] = last[:, half:]


def combine_out_kernel(
    z_ref, placing_ref, weight_ref, ids_ref, o_ref, g_ref, back_ref, *outs
):
    rows = o_ref.shape[0]
    placing = placing_ref[...].astype(F32)
    n = placing.shape[1]
    row_weight = weight_ref[:, 0:1]
    back_ref[...] = placing.T.astype(BF16)
    back_ref.send()
    weighted = (placing * row_weight).T
    hi = weighted.astype(BF16)
    lo = (weighted - hi.astype(F32)).astype(BF16)
    o = o_ref[...]
    inverse = jnp.where(row_weight > 0.0, 1.0 / jnp.where(row_weight > 0.0, row_weight, 1.0), 0.0)
    dots = jnp.sum(g_ref[...].astype(F32) * o.astype(F32), axis=1, keepdims=True) * inverse
    per_expert = jnp.sum(
        (placing * dots).reshape(PLANE, rows // PLANE, n), axis=1
    )
    expert = (lax.broadcasted_iota(jnp.int32, (PLANE, n), 0) * NZ + z_ref[0]).astype(F32)
    ids = ids_ref[...]
    probs = jnp.concatenate(
        [
            jnp.sum(jnp.where(ids[k : k + 1] == expert, per_expert, 0.0), axis=0, keepdims=True)
            for k in range(TOP)
        ],
        axis=0,
    )
    pieces = [v.astype(F32) for v in split3(probs)]
    pieces = jnp.concatenate([*pieces, jnp.zeros((128 - 3 * TOP, n), F32)], axis=0).T
    total = dot(hi, o) + dot(lo, o)
    put_parts(jnp.concatenate([total, pieces], axis=1), outs)


def combine_grads_kernel(back_ref, o_ref, *outs):
    put_parts(dot(back_ref[...], o_ref[...]), outs)


def forward_kernel(x_ref, wg_ref, wu_ref, wd_ref, slope_ref, swish_ref, hidden_ref, out_ref):
    x = x_ref[...]
    gate = dot(x, wg_ref[...])
    up = dot(x, wu_ref[...])
    squash = jax.nn.sigmoid(gate)
    swish = gate * squash
    hidden = (swish * up).astype(BF16)
    hidden_ref[...] = hidden
    hidden_ref.send()
    swish_ref[...] = swish
    swish_ref.send()
    slope_ref[...] = up * squash * (1.0 + gate * (1.0 - squash))
    slope_ref.send()
    for row in range(0, x_ref.shape[0], ROWS):
        here = slice(row, row + ROWS)
        out_ref[here] = dot(hidden[here], wd_ref[...]).astype(BF16)
        out_ref.send(here)


def backward_kernel(g_ref, wd_ref, slope_ref, swish_ref, wg_ref, wu_ref, gg_ref, ug_ref, dx_ref):
    hidden_grad = dot_nt(g_ref[...], wd_ref[...])
    gate_grad = (hidden_grad * slope_ref[...]).astype(BF16)
    gg_ref[...] = gate_grad
    gg_ref.send()
    up_grad = (hidden_grad * swish_ref[...]).astype(BF16)
    ug_ref[...] = up_grad
    ug_ref.send()
    for row in range(0, g_ref.shape[0], ROWS):
        here = slice(row, row + ROWS)
        part = dot_nt(gate_grad[here], wg_ref[...]) + dot_nt(up_grad[here], wu_ref[...])
        dx_ref[here] = part.astype(BF16)
        dx_ref.send(here)


def weight_grad_kernel(x_ref, pair_ref, hidden_ref, g_ref, *refs):
    received, (gu_ref, wd_ref) = refs[:-2], refs[-2:]
    f = hidden_ref.shape[1]
    for column in range(0, x_ref.shape[1], COLUMNS):
        here = slice(column, column + COLUMNS)
        v = dot_tn(x_ref[:, here], pair_ref[...])
        for i in range(2):
            one = v[:, i * f : (i + 1) * f]
            if received:
                one = one + received[0][i, here].astype(F32)
            gu_ref[i, here] = one.astype(BF16)
            gu_ref.send((i, here))
    v = dot_tn(hidden_ref[...], g_ref[...])
    if received:
        v = v + received[1][...].astype(F32)
    wd_ref[...] = v.astype(BF16)


def join_kernel(part_up, part_down, from_below, from_above, *refs):
    far, (up_ref, down_ref) = refs[:-2], refs[-2:]
    block = part_up.shape[0]
    up = part_up[...] + from_below[:block].astype(F32)
    down = part_down[...] + from_above[:block].astype(F32)
    half = far[0].shape[1]
    up_ref[:, :half] = (up[:, :half] + far[0][...].astype(F32)).astype(BF16)
    up_ref[:, half:] = up[:, half:].astype(BF16)
    down_ref[:, :half] = down[:, :half].astype(BF16)
    down_ref[:, half:] = (down[:, half:] + far[1][...].astype(F32)).astype(BF16)


def total_of(own, from_below, from_above, two_below, two_above):
    block = own.shape[0]
    total = own[...] + (from_below[block:].astype(F32) + from_above[block:].astype(F32))
    return total + (two_below[...].astype(F32) + two_above[...].astype(F32))


def finish_out_kernel(*refs):
    out_ref, prob_ref = refs[-2:]
    total = total_of(*refs[:-2])
    d = out_ref.shape[1]
    out_ref[...] = total[:, :d].astype(BF16)
    pieces = total[:, d:].T
    prob_ref[...] = pieces[0:TOP] + (pieces[TOP : 2 * TOP] + pieces[2 * TOP : 3 * TOP])


def finish_grads_kernel(*refs):
    refs[-1][...] = total_of(*refs[:-1]).astype(BF16)


def nothing_kernel(first, second, out):
    pass


def cost(flops, args, out_shapes):
    nbytes = sum(a.size * a.dtype.itemsize for a in [*args, *out_shapes])
    return pl.CostEstimate(flops=flops, bytes_accessed=nbytes, transcendentals=0)


class Arriving:
    def __init__(self, ref, copies):
        self.ref, self.copies, self.later = ref, copies, []
        self.shape, self.dtype = ref.shape, ref.dtype

    def start(self):
        for copy in self.copies:
            copy.start()

    def settle(self):
        for copy in self.copies:
            copy.wait()
        for buffer in self.later:
            buffer.start()
        self.copies, self.later = [], []

    def __getitem__(self, at):
        self.settle()
        return self.ref[at]


class Leaving:
    def __init__(self, ref, target, next_sem):
        self.ref, self.target, self.next_sem, self.copies = ref, target, next_sem, []
        self.shape, self.dtype = ref.shape, ref.dtype

    def __setitem__(self, at, value):
        self.ref[at] = value

    def send(self, at=None):
        source, target = (self.ref, self.target) if at is None else (self.ref.at[at], self.target.at[at])
        copy = pltpu.make_async_copy(source, target, self.next_sem())
        copy.start()
        self.copies.append(copy)


MOST_SENDS = 16


def staged(kernel, scalars, near, read, unread, loads, eager, made, *refs):
    first, rest = refs[: scalars + near], refs[scalars + near :]
    ins, rest = rest[:read], rest[read + unread :]
    outs, rest = rest[:made], rest[made:]
    held, rest = rest[: len(loads)], rest[len(loads) :]
    made_here, (in_sems, out_sems) = rest[:-2], rest[-2:]
    arriving, count = [], 0
    for here, (_, _, pieces) in zip(held, loads):
        copies = []
        for operand, source_at, target_at in pieces:
            source = ins[operand] if source_at is None else ins[operand].at[source_at]
            target = here if target_at is None else here.at[target_at]
            copies.append(pltpu.make_async_copy(source, target, in_sems.at[count]))
            count += 1
        arriving.append(Arriving(here, copies))
    for buffer in arriving[:eager]:
        buffer.start()
    if arriving[eager:]:
        arriving[eager - 1].later = arriving[eager:]
    sems = iter(range(MOST_SENDS))
    leaving = [Leaving(h, o, lambda: out_sems.at[next(sems)]) for h, o in zip(made_here, outs)]
    kernel(*first, *arriving, *(leaving or outs))
    for buffer in leaving:
        if not buffer.copies:
            buffer.send()
    for buffer in arriving:
        buffer.settle()
    for buffer in leaving:
        for copy in buffer.copies:
            copy.wait()


def call(
    kernel, out_shapes, args, scalars=0, near=0, unread=0, loads=None, eager=99, flops=0, vmem=63,
    near_out=False
):
    smem = pl.BlockSpec(memory_space=pltpu.SMEM)
    whole = pl.BlockSpec(memory_space=pltpu.VMEM)
    hbm = pl.BlockSpec(memory_space=pl.ANY)
    shapes = [jax.ShapeDtypeStruct(s, t) for s, t in out_shapes]
    read = len(args) - scalars - near - unread
    ins = args[scalars + near : scalars + near + read]
    if loads is None:
        loads = [(a.shape, a.dtype, [(i, None, None)]) for i, a in enumerate(ins)]
    copies = sum(len(pieces) for _, _, pieces in loads)
    counted = args[scalars : len(args) - unread] if flops else []
    return pl.pallas_call(
        functools.partial(
            staged, kernel, scalars, near, read, unread, loads, eager, len(shapes)
        ),
        out_shape=shapes,
        in_specs=[smem] * scalars + [whole] * near + [hbm] * (read + unread),
        out_specs=[whole if near_out else hbm] * len(shapes),
        scratch_shapes=[pltpu.VMEM(shape, dtype) for shape, dtype, _ in loads]
        + [pltpu.VMEM(a.shape, a.dtype) for a in shapes if not near_out]
        + [pltpu.SemaphoreType.DMA((copies,)), pltpu.SemaphoreType.DMA((MOST_SENDS,))],
        compiler_params=pltpu.CompilerParams(vmem_limit_bytes=vmem * MIB),
        cost_estimate=cost(flops, counted, shapes if flops else []),
    )(*args)


def dropping(kernel, read, unread, *refs):
    kernel(*refs[:read], *refs[read + unread :])


def small(kernel, out_shapes, args, unread=0, vmem=8, flops=0):
    whole = pl.BlockSpec(memory_space=pltpu.VMEM)
    hbm = pl.BlockSpec(memory_space=pl.ANY)
    shapes = [jax.ShapeDtypeStruct(s, t) for s, t in out_shapes]
    read = len(args) - unread
    return pl.pallas_call(
        functools.partial(dropping, kernel, read, unread),
        out_shape=shapes,
        in_specs=[whole] * read + [hbm] * unread,
        out_specs=[whole] * len(shapes),
        compiler_params=pltpu.CompilerParams(vmem_limit_bytes=vmem * MIB),
        cost_estimate=cost(flops, args[:read], shapes),
    )(*args)


def beside(shape, one, other, at=None):
    width = shape[1]
    return (
        (shape[0], 2 * width),
        BF16,
        [
            (one, at, (slice(None), slice(0, width))),
            (other, at, (slice(None), slice(width, 2 * width))),
        ],
    )


def below(shape, one, other):
    height = shape[0]
    return (
        (2 * height, shape[1]),
        BF16,
        [(one, None, slice(0, height)), (other, None, slice(height, 2 * height))],
    )


def forward(x, gu, wd):
    rows, d = x.shape
    f = wd[0].shape[0]
    wide = (rows, 2 * f)
    return call(
        forward_kernel,
        [(wide, F32), (wide, F32), (wide, BF16), ((rows, d), BF16)],
        [x, *gu, *wd],
        loads=[
            (x.shape, BF16, [(0, None, None)]),
            beside((d, f), 1, 2, 0),
            beside((d, f), 1, 2, 1),
            below((f, d), 3, 4),
        ],
        flops=12 * rows * d * f,
    )


def backward(g, slope, swish, gu, wd):
    rows, d = g.shape
    f = wd[0].shape[0]
    return call(
        backward_kernel,
        [((rows, 2 * f), BF16), ((rows, 2 * f), BF16), ((rows, d), BF16)],
        [g, slope, swish, *gu, *wd],
        loads=[
            (g.shape, BF16, [(0, None, None)]),
            below((f, d), 5, 6),
            (slope.shape, F32, [(1, None, None)]),
            (swish.shape, F32, [(2, None, None)]),
            beside((d, f), 3, 4, 0),
            beside((d, f), 3, 4, 1),
        ],
        flops=12 * rows * d * f,
    )


def weight_grads(x, g, gg, ug, hidden, half, received=()):
    rows, d = x.shape
    f = gg.shape[1] // 2
    mine = (slice(None), slice(half * f, (half + 1) * f))
    pair = [(2, mine, (slice(None), slice(0, f))), (3, mine, (slice(None), slice(f, 2 * f)))]
    return call(
        weight_grad_kernel,
        [((2, d, f), BF16), ((f, d), BF16)],
        [x, g, gg, ug, hidden, *received],
        loads=[
            (x.shape, BF16, [(0, None, None)]),
            ((rows, 2 * f), BF16, pair),
            ((rows, f), BF16, [(4, mine, None)]),
            (g.shape, BF16, [(1, None, None)]),
        ]
        + [(v.shape, BF16, [(5 + i, None, None)]) for i, v in enumerate(received)],
        flops=0 if received else 6 * rows * d * f,
    )


def after(value, earlier):
    hbm = pl.BlockSpec(memory_space=pl.ANY)
    return pl.pallas_call(
        nothing_kernel,
        out_shape=jax.ShapeDtypeStruct(value.shape, value.dtype),
        in_specs=[hbm, hbm],
        out_specs=hbm,
        input_output_aliases={0: 0},
        cost_estimate=pl.CostEstimate(flops=0, bytes_accessed=0, transcendentals=0),
    )(value, earlier)


def shift_z(v, step):
    return lax.ppermute(v, "z", [(i, (i + step) % NZ) for i in range(NZ)])


def gather_z(own):
    held = {0: own}
    for hop in range(1, 5):
        if hop < 4:
            held[-hop] = shift_z(held[1 - hop], 1)
        held[hop] = shift_z(held[hop - 1], -1)
    return [held[r] for r in ORDER]


def part_shapes(t, width):
    half = (width // 2 + 127) // 128 * 128
    return (
        [((t, width), F32)] * 3
        + [((2 * t, width), BF16)] * 2
        + [((t, half), BF16), ((t, width - half), BF16)]
    )


def scatter_z(parts, finish, out_shapes, run, earlier=()):
    own, two_up, two_down, up, down, *far = parts
    from_below, from_above = shift_z(up, 1), shift_z(down, -1)
    far = [shift_z(v, step) for v, step in zip(far, (2, -2))]
    two_up, two_down = run(
        join_kernel,
        [(two_up.shape, BF16)] * 2,
        [two_up, two_down, from_below, from_above, *far, *earlier],
        unread=len(earlier),
    )
    two_below, two_above = shift_z(two_up, 2), shift_z(two_down, -2)
    return two_up, small(finish, out_shapes, [own, from_below, from_above, two_below, two_above])


def swap_dp(v):
    return lax.ppermute(v, "dp", [(0, 1), (1, 0)])


def exchange_plane(rows):
    r, d = rows.shape
    out = lax.all_to_all(
        rows.reshape(PLANE, r // PLANE, d), ("x", "y"), split_axis=0, concat_axis=0, tiled=True
    )
    return out.reshape(r, d)


def on_device(tokens, expert_ids, route_weight, w_gate_up, w_down, out_grad):
    t, d = tokens.shape[1:]
    n = t * NZ
    rows = PLANE * NZ * SLOTS
    z = lax.axis_index("z").astype(jnp.int32).reshape(1)

    gu = (w_gate_up[0], swap_dp(w_gate_up[0]))
    wd = (w_down[0], swap_dp(w_down[0]))
    (blob,) = call(
        blob_kernel,
        [((t, d + 128), BF16)],
        [expert_ids[0].T, route_weight[0].T, tokens[0]],
        near_out=True,
        vmem=62,
    )
    blobs = gather_z(blob)
    send_x, placing, row_weight, ids = call(
        place_tokens_kernel,
        [((rows, d), BF16), ((rows, n), BF16), ((rows, 128), F32), ((TOP, n), F32)],
        [z, *blobs, gu[1], wd[1]],
        scalars=1,
        near=NZ,
        unread=2,
        vmem=62,
        flops=2 * rows * n * d,
    )
    x = exchange_plane(send_x)
    grads = gather_z(out_grad[0])
    (send_g,) = call(
        place_grads_kernel,
        [((rows, d), BF16)],
        [*grads, placing, row_weight],
        near=NZ + 2,
        flops=2 * rows * n * d,
        vmem=62,
    )
    g = exchange_plane(send_g)
    slope, swish, hidden, out_rows = forward(x, gu, wd)
    o = exchange_plane(after(out_rows, g))
    gate_grad, up_grad, grad_rows = backward(g, slope, swish, gu, wd)
    grad_rows = after(grad_rows, o)
    dx = exchange_plane(grad_rows)

    away = weight_grads(x, g, gate_grad, up_grad, hidden, 1)
    received = [swap_dp(v) for v in away]
    grad_gate_up, grad_down = weight_grads(x, g, gate_grad, up_grad, hidden, 0, received)

    back, *parts = call(
        combine_out_kernel,
        [((n, rows), BF16)] + part_shapes(t, d + 128),
        [z, placing, row_weight, ids, o, send_g, away[0], grad_rows],
        scalars=1,
        unread=2,
    )
    midway, (layer_out, prob_grad) = scatter_z(
        parts, finish_out_kernel, [((t, d), BF16), ((TOP, t), F32)], call, [grad_gate_up]
    )
    parts = call(
        combine_grads_kernel,
        part_shapes(t, d),
        [back, after(dx, midway)],
        near=1,
        near_out=True,
        vmem=48,
        flops=2 * rows * n * d,
    )
    _, (token_grad,) = scatter_z(parts, finish_grads_kernel, [((t, d), BF16)], small)
    return (
        layer_out[None],
        token_grad[None],
        prob_grad.T[None],
        grad_gate_up[None],
        grad_down[None],
    )


def solution(mesh):
    fine = Mesh(mesh.devices.reshape(NX, NY, NZ, 2), ("x", "y", "z", "dp"))
    expert = ("x", "y", "z")
    by_token = P("dp", expert, None)
    specs = (by_token, by_token, by_token, P(expert, None, None, "dp"), P(expert, "dp", None))
    return jax.shard_map(
        on_device,
        mesh=fine,
        in_specs=specs + (by_token,),
        out_specs=(by_token, by_token, by_token, specs[3], specs[4]),
        check_vma=False,
    )
```

```python
import functools

import jax
import jax.numpy as jnp
import numpy as np
from jax import lax
from jax.experimental import pallas as pl
from jax.experimental.pallas import tpu as pltpu
from jax.sharding import Mesh, PartitionSpec as P

F32 = jnp.float32
BF16 = jnp.bfloat16
NX, NY, NZ = 4, 4, 8
PLANE = NX * NY
SLOTS = 4
TOP = 8
MIB = 1 << 20
ROWS = 256
COLUMNS = 2048


def dot(a, b):
    return jnp.dot(a, b, preferred_element_type=F32)


def dot_nt(a, b):
    return lax.dot_general(a, b, (((1,), (1,)), ((), ())), preferred_element_type=F32)


def dot_tn(a, b):
    return lax.dot_general(a, b, (((0,), (0,)), ((), ())), preferred_element_type=F32)


def split3(v):
    hi = v.astype(BF16)
    rest = v - hi.astype(F32)
    mid = rest.astype(BF16)
    lo = (rest - mid.astype(F32)).astype(BF16)
    return hi, mid, lo


ORDER = (0, -1, 1, -2, 2, -3, 3, 4)


def place(meta, z):
    n = meta.shape[0]
    rows = PLANE * NZ * SLOTS
    turned = meta.T
    ids = turned[0:TOP]
    weights = turned[TOP : 2 * TOP] + turned[2 * TOP : 3 * TOP] + turned[3 * TOP : 4 * TOP]
    expert = (lax.broadcasted_iota(jnp.int32, (PLANE, n), 0) * NZ + z).astype(F32)
    named = jnp.zeros((PLANE, n), F32)
    weight = jnp.zeros((PLANE, n), F32)
    for k in range(TOP):
        hit = ids[k : k + 1] == expert
        named = jnp.where(hit, 1.0, named)
        weight = jnp.where(hit, weights[k : k + 1], weight)
    block = n // NZ
    shift = block.bit_length() - 1
    from_t = lax.broadcasted_iota(jnp.int32, (n, n), 0)
    to_t = lax.broadcasted_iota(jnp.int32, (n, n), 1)
    same = lax.shift_right_logical(from_t, shift) == lax.shift_right_logical(to_t, shift)
    before = jnp.where(same & (from_t < to_t), 1.0, 0.0).astype(BF16)
    rank = dot(named.astype(BF16), before)
    rank = jnp.where(named > 0.5, rank, -1.0)

    def spread(v):
        return jnp.broadcast_to(v[:, None, :], (PLANE, NZ * SLOTS, n)).reshape(rows, n)

    row = lax.broadcasted_iota(jnp.int32, (rows, n), 0)
    col = lax.broadcasted_iota(jnp.int32, (rows, n), 1)
    row_block = lax.shift_right_logical(row, 2) & (NZ - 1)
    slot = (row & (SLOTS - 1)).astype(F32)
    here = (spread(rank) == slot) & (lax.shift_right_logical(col, shift) == row_block)
    placing = jnp.where(here, 1.0, 0.0)
    row_weight = jnp.sum(jnp.where(here, spread(weight), 0.0), axis=1, keepdims=True)
    return placing, row_weight, ids


def blob_kernel(ids_ref, weight_ref, tokens_ref, blob_ref):
    t, d = tokens_ref.shape
    pieces = [v.astype(F32) for v in split3(weight_ref[...])]
    rest = jnp.zeros((128 - 4 * TOP, t), F32)
    meta = jnp.concatenate([ids_ref[...].astype(F32), *pieces, rest], axis=0)
    blob_ref[:, :d] = tokens_ref[...]
    blob_ref[:, d:] = meta.T.astype(BF16)


def place_tokens_kernel(z_ref, *refs):
    blobs, (x_ref, placing_ref, weight_ref, ids_ref) = refs[:NZ], refs[NZ:]
    d = x_ref.shape[1]
    meta = jnp.concatenate([b[:, d:].astype(F32) for b in blobs], axis=0)
    placing, row_weight, ids = place(meta, z_ref[0])
    placing = placing.astype(BF16)
    placing_ref[...] = placing
    weight_ref[...] = jnp.broadcast_to(row_weight, weight_ref.shape)
    ids_ref[...] = ids
    for ref in (placing_ref, weight_ref, ids_ref):
        ref.send()
    tokens = jnp.concatenate([b[:, :d] for b in blobs], axis=0)
    for row in range(0, x_ref.shape[0], ROWS):
        here = slice(row, row + ROWS)
        x_ref[here] = dot(placing[here], tokens).astype(BF16)
        x_ref.send(here)


def place_grads_kernel(*refs):
    grads, (placing_ref, weight_ref, g_ref) = refs[:NZ], refs[NZ:]
    placing = placing_ref[...]
    og = jnp.concatenate([b[...] for b in grads], axis=0)
    for row in range(0, g_ref.shape[0], ROWS):
        here = slice(row, row + ROWS)
        g_ref[here] = (dot(placing[here], og) * weight_ref[here, 0:1]).astype(BF16)
        g_ref.send(here)


def put_parts(total, outs):
    block = total.shape[0] // NZ
    part = {r: total[i * block : (i + 1) * block] for i, r in enumerate(ORDER)}
    own, two_up, two_down, up, down, *far = outs
    half = far[0].shape[1]
    own[...] = part[0]
    two_up[...] = part[2]
    two_down[...] = part[-2]
    for out, sign in ((up, 1), (down, -1)):
        out[:block] = part[3 * sign].astype(BF16)
        out[block:] = part[sign].astype(BF16)
    last = part[4].astype(BF16)
    far[0][...] = last[:, :half]
    far[1][...] = last[:, half:]


def combine_out_kernel(
    z_ref, placing_ref, weight_ref, ids_ref, o_ref, g_ref, back_ref, *outs
):
    rows = o_ref.shape[0]
    placing = placing_ref[...].astype(F32)
    n = placing.shape[1]
    row_weight = weight_ref[:, 0:1]
    back_ref[...] = placing.T.astype(BF16)
    back_ref.send()
    weighted = (placing * row_weight).T
    hi = weighted.astype(BF16)
    lo = (weighted - hi.astype(F32)).astype(BF16)
    o = o_ref[...]
    inverse = jnp.where(row_weight > 0.0, 1.0 / jnp.where(row_weight > 0.0, row_weight, 1.0), 0.0)
    dots = jnp.sum(g_ref[...].astype(F32) * o.astype(F32), axis=1, keepdims=True) * inverse
    per_expert = jnp.sum(
        (placing * dots).reshape(PLANE, rows // PLANE, n), axis=1
    )
    expert = (lax.broadcasted_iota(jnp.int32, (PLANE, n), 0) * NZ + z_ref[0]).astype(F32)
    ids = ids_ref[...]
    probs = jnp.concatenate(
        [
            jnp.sum(jnp.where(ids[k : k + 1] == expert, per_expert, 0.0), axis=0, keepdims=True)
            for k in range(TOP)
        ],
        axis=0,
    )
    pieces = [v.astype(F32) for v in split3(probs)]
    pieces = jnp.concatenate([*pieces, jnp.zeros((128 - 3 * TOP, n), F32)], axis=0).T
    total = dot(hi, o) + dot(lo, o)
    put_parts(jnp.concatenate([total, pieces], axis=1), outs)


def combine_grads_kernel(back_ref, o_ref, *outs):
    put_parts(dot(back_ref[...], o_ref[...]), outs)


def forward_kernel(x_ref, wg_ref, wu_ref, wd_ref, slope_ref, swish_ref, hidden_ref, out_ref):
    x = x_ref[...]
    gate = dot(x, wg_ref[...])
    up = dot(x, wu_ref[...])
    squash = jax.nn.sigmoid(gate)
    swish = gate * squash
    hidden = (swish * up).astype(BF16)
    hidden_ref[...] = hidden
    hidden_ref.send()
    swish_ref[...] = swish
    swish_ref.send()
    slope_ref[...] = up * squash * (1.0 + gate * (1.0 - squash))
    slope_ref.send()
    for row in range(0, x_ref.shape[0], ROWS):
        here = slice(row, row + ROWS)
        out_ref[here] = dot(hidden[here], wd_ref[...]).astype(BF16)
        out_ref.send(here)


def backward_kernel(g_ref, wd_ref, slope_ref, swish_ref, wg_ref, wu_ref, gg_ref, ug_ref, dx_ref):
    hidden_grad = dot_nt(g_ref[...], wd_ref[...])
    gate_grad = (hidden_grad * slope_ref[...]).astype(BF16)
    gg_ref[...] = gate_grad
    gg_ref.send()
    up_grad = (hidden_grad * swish_ref[...]).astype(BF16)
    ug_ref[...] = up_grad
    ug_ref.send()
    for row in range(0, g_ref.shape[0], ROWS):
        here = slice(row, row + ROWS)
        part = dot_nt(gate_grad[here], wg_ref[...]) + dot_nt(up_grad[here], wu_ref[...])
        dx_ref[here] = part.astype(BF16)
        dx_ref.send(here)


def weight_grad_kernel(x_ref, pair_ref, hidden_ref, g_ref, *refs):
    received, (gu_ref, wd_ref) = refs[:-2], refs[-2:]
    f = hidden_ref.shape[1]
    for column in range(0, x_ref.shape[1], COLUMNS):
        here = slice(column, column + COLUMNS)
        v = dot_tn(x_ref[:, here], pair_ref[...])
        for i in range(2):
            one = v[:, i * f : (i + 1) * f]
            if received:
                one = one + received[0][i, here].astype(F32)
            gu_ref[i, here] = one.astype(BF16)
            gu_ref.send((i, here))
    v = dot_tn(hidden_ref[...], g_ref[...])
    if received:
        v = v + received[1][...].astype(F32)
    wd_ref[...] = v.astype(BF16)


def join_kernel(part_up, part_down, from_below, from_above, *refs):
    far, (up_ref, down_ref) = refs[:-2], refs[-2:]
    block = part_up.shape[0]
    up = part_up[...] + from_below[:block].astype(F32)
    down = part_down[...] + from_above[:block].astype(F32)
    half = far[0].shape[1]
    up_ref[:, :half] = (up[:, :half] + far[0][...].astype(F32)).astype(BF16)
    up_ref[:, half:] = up[:, half:].astype(BF16)
    down_ref[:, :half] = down[:, :half].astype(BF16)
    down_ref[:, half:] = (down[:, half:] + far[1][...].astype(F32)).astype(BF16)


def total_of(own, from_below, from_above, two_below, two_above):
    block = own.shape[0]
    total = own[...] + (from_below[block:].astype(F32) + from_above[block:].astype(F32))
    return total + (two_below[...].astype(F32) + two_above[...].astype(F32))


def finish_out_kernel(*refs):
    out_ref, prob_ref = refs[-2:]
    total = total_of(*refs[:-2])
    d = out_ref.shape[1]
    out_ref[...] = total[:, :d].astype(BF16)
    pieces = total[:, d:].T
    prob_ref[...] = pieces[0:TOP] + (pieces[TOP : 2 * TOP] + pieces[2 * TOP : 3 * TOP])


def finish_grads_kernel(*refs):
    refs[-1][...] = total_of(*refs[:-1]).astype(BF16)


def nothing_kernel(first, second, out):
    pass


def cost(flops, args, out_shapes):
    nbytes = sum(a.size * a.dtype.itemsize for a in [*args, *out_shapes])
    return pl.CostEstimate(flops=flops, bytes_accessed=nbytes, transcendentals=0)


class Arriving:
    def __init__(self, ref, copies):
        self.ref, self.copies, self.later = ref, copies, []
        self.shape, self.dtype = ref.shape, ref.dtype

    def start(self):
        for copy in self.copies:
            copy.start()

    def settle(self):
        for copy in self.copies:
            copy.wait()
        for buffer in self.later:
            buffer.start()
        self.copies, self.later = [], []

    def __getitem__(self, at):
        self.settle()
        return self.ref[at]


class Leaving:
    def __init__(self, ref, target, next_sem):
        self.ref, self.target, self.next_sem, self.copies = ref, target, next_sem, []
        self.shape, self.dtype = ref.shape, ref.dtype

    def __setitem__(self, at, value):
        self.ref[at] = value

    def send(self, at=None):
        source, target = (self.ref, self.target) if at is None else (self.ref.at[at], self.target.at[at])
        copy = pltpu.make_async_copy(source, target, self.next_sem())
        copy.start()
        self.copies.append(copy)


MOST_SENDS = 16


def staged(kernel, scalars, near, read, unread, loads, eager, made, *refs):
    first, rest = refs[: scalars + near], refs[scalars + near :]
    ins, rest = rest[:read], rest[read + unread :]
    outs, rest = rest[:made], rest[made:]
    held, rest = rest[: len(loads)], rest[len(loads) :]
    made_here, (in_sems, out_sems) = rest[:-2], rest[-2:]
    arriving, count = [], 0
    for here, (_, _, pieces) in zip(held, loads):
        copies = []
        for operand, source_at, target_at in pieces:
            source = ins[operand] if source_at is None else ins[operand].at[source_at]
            target = here if target_at is None else here.at[target_at]
            copies.append(pltpu.make_async_copy(source, target, in_sems.at[count]))
            count += 1
        arriving.append(Arriving(here, copies))
    for buffer in arriving[:eager]:
        buffer.start()
    if arriving[eager:]:
        arriving[eager - 1].later = arriving[eager:]
    sems = iter(range(MOST_SENDS))
    leaving = [Leaving(h, o, lambda: out_sems.at[next(sems)]) for h, o in zip(made_here, outs)]
    kernel(*first, *arriving, *(leaving or outs))
    for buffer in leaving:
        if not buffer.copies:
            buffer.send()
    for buffer in arriving:
        buffer.settle()
    for buffer in leaving:
        for copy in buffer.copies:
            copy.wait()


def call(
    kernel, out_shapes, args, scalars=0, near=0, unread=0, loads=None, eager=99, flops=0, vmem=63,
    near_out=False
):
    smem = pl.BlockSpec(memory_space=pltpu.SMEM)
    whole = pl.BlockSpec(memory_space=pltpu.VMEM)
    hbm = pl.BlockSpec(memory_space=pl.ANY)
    shapes = [jax.ShapeDtypeStruct(s, t) for s, t in out_shapes]
    read = len(args) - scalars - near - unread
    ins = args[scalars + near : scalars + near + read]
    if loads is None:
        loads = [(a.shape, a.dtype, [(i, None, None)]) for i, a in enumerate(ins)]
    copies = sum(len(pieces) for _, _, pieces in loads)
    counted = args[scalars : len(args) - unread] if flops else []
    return pl.pallas_call(
        functools.partial(
            staged, kernel, scalars, near, read, unread, loads, eager, len(shapes)
        ),
        out_shape=shapes,
        in_specs=[smem] * scalars + [whole] * near + [hbm] * (read + unread),
        out_specs=[whole if near_out else hbm] * len(shapes),
        scratch_shapes=[pltpu.VMEM(shape, dtype) for shape, dtype, _ in loads]
        + [pltpu.VMEM(a.shape, a.dtype) for a in shapes if not near_out]
        + [pltpu.SemaphoreType.DMA((copies,)), pltpu.SemaphoreType.DMA((MOST_SENDS,))],
        compiler_params=pltpu.CompilerParams(vmem_limit_bytes=vmem * MIB),
        cost_estimate=cost(flops, counted, shapes if flops else []),
    )(*args)


def dropping(kernel, read, unread, *refs):
    kernel(*refs[:read], *refs[read + unread :])


def small(kernel, out_shapes, args, unread=0, vmem=8, flops=0):
    whole = pl.BlockSpec(memory_space=pltpu.VMEM)
    hbm = pl.BlockSpec(memory_space=pl.ANY)
    shapes = [jax.ShapeDtypeStruct(s, t) for s, t in out_shapes]
    read = len(args) - unread
    return pl.pallas_call(
        functools.partial(dropping, kernel, read, unread),
        out_shape=shapes,
        in_specs=[whole] * read + [hbm] * unread,
        out_specs=[whole] * len(shapes),
        compiler_params=pltpu.CompilerParams(vmem_limit_bytes=vmem * MIB),
        cost_estimate=cost(flops, args[:read], shapes),
    )(*args)


def beside(shape, one, other, at=None):
    width = shape[1]
    return (
        (shape[0], 2 * width),
        BF16,
        [
            (one, at, (slice(None), slice(0, width))),
            (other, at, (slice(None), slice(width, 2 * width))),
        ],
    )


def below(shape, one, other):
    height = shape[0]
    return (
        (2 * height, shape[1]),
        BF16,
        [(one, None, slice(0, height)), (other, None, slice(height, 2 * height))],
    )


def forward(x, gu, wd):
    rows, d = x.shape
    f = wd[0].shape[0]
    wide = (rows, 2 * f)
    return call(
        forward_kernel,
        [(wide, F32), (wide, F32), (wide, BF16), ((rows, d), BF16)],
        [x, *gu, *wd],
        loads=[
            (x.shape, BF16, [(0, None, None)]),
            beside((d, f), 1, 2, 0),
            beside((d, f), 1, 2, 1),
            below((f, d), 3, 4),
        ],
        flops=12 * rows * d * f,
    )


def backward(g, slope, swish, gu, wd):
    rows, d = g.shape
    f = wd[0].shape[0]
    return call(
        backward_kernel,
        [((rows, 2 * f), BF16), ((rows, 2 * f), BF16), ((rows, d), BF16)],
        [g, slope, swish, *gu, *wd],
        loads=[
            (g.shape, BF16, [(0, None, None)]),
            below((f, d), 5, 6),
            (slope.shape, F32, [(1, None, None)]),
            (swish.shape, F32, [(2, None, None)]),
            beside((d, f), 3, 4, 0),
            beside((d, f), 3, 4, 1),
        ],
        flops=12 * rows * d * f,
    )


def weight_grads(x, g, gg, ug, hidden, half, received=()):
    rows, d = x.shape
    f = gg.shape[1] // 2
    mine = (slice(None), slice(half * f, (half + 1) * f))
    pair = [(2, mine, (slice(None), slice(0, f))), (3, mine, (slice(None), slice(f, 2 * f)))]
    return call(
        weight_grad_kernel,
        [((2, d, f), BF16), ((f, d), BF16)],
        [x, g, gg, ug, hidden, *received],
        loads=[
            (x.shape, BF16, [(0, None, None)]),
            ((rows, 2 * f), BF16, pair),
            ((rows, f), BF16, [(4, mine, None)]),
            (g.shape, BF16, [(1, None, None)]),
        ]
        + [(v.shape, BF16, [(5 + i, None, None)]) for i, v in enumerate(received)],
        flops=0 if received else 6 * rows * d * f,
    )


def after(value, earlier):
    hbm = pl.BlockSpec(memory_space=pl.ANY)
    return pl.pallas_call(
        nothing_kernel,
        out_shape=jax.ShapeDtypeStruct(value.shape, value.dtype),
        in_specs=[hbm, hbm],
        out_specs=hbm,
        input_output_aliases={0: 0},
        cost_estimate=pl.CostEstimate(flops=0, bytes_accessed=0, transcendentals=0),
    )(value, earlier)


def shift_z(v, step):
    return lax.ppermute(v, "z", [(i, (i + step) % NZ) for i in range(NZ)])


def gather_z(own):
    held = {0: own}
    for hop in range(1, 5):
        if hop < 4:
            held[-hop] = shift_z(held[1 - hop], 1)
        held[hop] = shift_z(held[hop - 1], -1)
    return [held[r] for r in ORDER]


def part_shapes(t, width):
    half = (width // 2 + 127) // 128 * 128
    return (
        [((t, width), F32)] * 3
        + [((2 * t, width), BF16)] * 2
        + [((t, half), BF16), ((t, width - half), BF16)]
    )


def scatter_z(parts, finish, out_shapes, run, earlier=()):
    own, two_up, two_down, up, down, *far = parts
    from_below, from_above = shift_z(up, 1), shift_z(down, -1)
    far = [shift_z(v, step) for v, step in zip(far, (2, -2))]
    two_up, two_down = run(
        join_kernel,
        [(two_up.shape, BF16)] * 2,
        [two_up, two_down, from_below, from_above, *far, *earlier],
        unread=len(earlier),
    )
    two_below, two_above = shift_z(two_up, 2), shift_z(two_down, -2)
    return two_up, small(finish, out_shapes, [own, from_below, from_above, two_below, two_above])


def swap_dp(v):
    return lax.ppermute(v, "dp", [(0, 1), (1, 0)])


def exchange_plane(rows):
    r, d = rows.shape
    out = lax.all_to_all(
        rows.reshape(PLANE, r // PLANE, d), ("x", "y"), split_axis=0, concat_axis=0, tiled=True
    )
    return out.reshape(r, d)


def on_device(tokens, expert_ids, route_weight, w_gate_up, w_down, out_grad):
    t, d = tokens.shape[1:]
    n = t * NZ
    rows = PLANE * NZ * SLOTS
    z = lax.axis_index("z").astype(jnp.int32).reshape(1)

    gu = (w_gate_up[0], swap_dp(w_gate_up[0]))
    wd = (w_down[0], swap_dp(w_down[0]))
    (blob,) = call(
        blob_kernel,
        [((t, d + 128), BF16)],
        [expert_ids[0].T, route_weight[0].T, tokens[0]],
    )
    blobs = gather_z(blob)
    send_x, placing, row_weight, ids = call(
        place_tokens_kernel,
        [((rows, d), BF16), ((rows, n), BF16), ((rows, 128), F32), ((TOP, n), F32)],
        [z, *blobs, gu[1], wd[1]],
        scalars=1,
        near=NZ,
        unread=2,
        vmem=62,
        flops=2 * rows * n * d,
    )
    x = exchange_plane(send_x)
    grads = gather_z(out_grad[0])
    (send_g,) = call(
        place_grads_kernel,
        [((rows, d), BF16)],
        [*grads, placing, row_weight],
        near=NZ + 2,
        flops=2 * rows * n * d,
        vmem=62,
    )
    g = exchange_plane(send_g)
    slope, swish, hidden, out_rows = forward(x, gu, wd)
    o = exchange_plane(after(out_rows, g))
    gate_grad, up_grad, grad_rows = backward(g, slope, swish, gu, wd)
    grad_rows = after(grad_rows, o)
    dx = exchange_plane(grad_rows)

    away = weight_grads(x, g, gate_grad, up_grad, hidden, 1)
    received = [swap_dp(v) for v in away]
    grad_gate_up, grad_down = weight_grads(x, g, gate_grad, up_grad, hidden, 0, received)

    back, *parts = call(
        combine_out_kernel,
        [((n, rows), BF16)] + part_shapes(t, d + 128),
        [z, placing, row_weight, ids, o, send_g, away[0], grad_rows],
        scalars=1,
        unread=2,
    )
    midway, (layer_out, prob_grad) = scatter_z(
        parts, finish_out_kernel, [((t, d), BF16), ((TOP, t), F32)], call, [grad_gate_up]
    )
    parts = call(
        combine_grads_kernel,
        part_shapes(t, d),
        [back, after(dx, midway)],
        near=1,
        near_out=True,
        vmem=48,
        flops=2 * rows * n * d,
    )
    _, (token_grad,) = scatter_z(parts, finish_grads_kernel, [((t, d), BF16)], small)
    return (
        layer_out[None],
        token_grad[None],
        prob_grad.T[None],
        grad_gate_up[None],
        grad_down[None],
    )


def solution(mesh):
    fine = Mesh(mesh.devices.reshape(NX, NY, NZ, 2), ("x", "y", "z", "dp"))
    expert = ("x", "y", "z")
    by_token = P("dp", expert, None)
    specs = (by_token, by_token, by_token, P(expert, None, None, "dp"), P(expert, "dp", None))
    return jax.shard_map(
        on_device,
        mesh=fine,
        in_specs=specs + (by_token,),
        out_specs=(by_token, by_token, by_token, specs[3], specs[4]),
        check_vma=False,
    )
```
